128 devices in a mesh: blk: 8 (over x, core), line: 16 (over z, y).
Axes of the slice: x: 4, y: 4, z: 4, core: 2. Of those that a mesh axis runs over, the one named last changes fastest.
Arguments:
- state: float32 [8, 5, 256, 64, 128], P('blk', None, None, 'line'), may hold values from -6 to 6
- first_flux: float32 [8, 5, 5], P('blk'), may hold values from -1.25 to 1.25
- second_flux: float32 [8, 5, 5], P('blk'), may hold values from -1.25 to 1.25
- viscosity: float32 [8], P('blk'), may hold values from 0.02 to 0.15
- first_inverse: float32 [8, 256, 256], P('blk'), may hold values from 0 to 1.7
- second_inverse: float32 [8, 64, 64], P('blk'), may hold values from 0 to 1.7
- donor_cell: int32 [128, 128, 128], P(('blk', 'line')), may hold values from 0 to 131070, as said below
- donor_weight: float32 [128, 128, 128], P(('blk', 'line')), may hold values from 0 to 1
- receptor_cell: int32 [128, 128, 128], P(('blk', 'line')), may hold values from 0 to 131072, as said below
Outputs:
- advanced: float32 [8, 5, 256, 64, 128], P('blk', None, None, 'line')
The draws below stay inside these ranges and needn't reach their ends.
Inputs may be any that keep to these rules, and one draw needn't show every extreme that they name: `donor_cell`: entry [n, m, p] is a local cell index of sending piece n whose third-direction index is below 127. `receptor_cell`: entry [m, n, p] is the local cell of receiving piece m that takes slot p from sending piece n, or 131072 where the slot is unused; the used cells of one receiving piece are distinct; pieces of the same block exchange nothing; every receiving piece has one sending piece whose 128 slots are all used.
All inputs are finite; a program needn't handle non-finite values.
Results may differ from the reference program's by a relative error of at most 0.0003.
Values sent between devices are 32-bit elements; how exact they have to be, the bound alone decides.
No kernel may reach another device: no remote copies, remote signals or barrier semaphores. Data moves between devices by JAX's collectives and lax.ppermute only.
A program may use at most 256 MiB of HBM per device.

```python
import math
import jax
import jax.numpy as jnp
from jax import lax

VARS = 5
NI = 256
CJ = 4
NK = 128
P_SIZE = 128
ITERS = 1
BLOCKS = 8
RANGES = 16
PIECES = 128
NJ = 64


def decay_operator(base_key, order, span_cells):
    key_decay, key_diagonal, key_jitter = jax.random.split(base_key, 3)
    decay_rate = jnp.exp(jax.random.uniform(key_decay, (BLOCKS,), jnp.float32, jnp.log(0.15), jnp.log(0.6)))
    diagonal = jax.random.uniform(key_diagonal, (BLOCKS, order), jnp.float32, 0.7, 1.3)
    jitter_factor = 1.0 + 0.3 * jnp.clip(jax.random.normal(key_jitter, (BLOCKS, order, order), jnp.float32), -1.3, 1.3)
    step_ratio = jnp.exp(-decay_rate / span_cells)
    positions = jnp.arange(order, dtype=jnp.float32)
    distance = jnp.abs(positions[:, None] - positions[None, :])
    tail_part = 0.5 * ((1.0 - step_ratio) / (1.0 + step_ratio))[:, None, None]
    tail_part = tail_part * jnp.exp(-distance[None, :, :] * (decay_rate / span_cells)[:, None, None]) * jitter_factor
    return tail_part + diagonal[:, :, None] * jnp.eye(order, dtype=jnp.float32)[None, :, :]


def draw_first_inverse(key, part):
    return decay_operator(jax.random.fold_in(key, 11), NI, NI // 4)


def draw_second_inverse(key, part):
    return decay_operator(jax.random.fold_in(key, 12), NJ, CJ)


def draw_donor_cell(key, part):
    picked = jax.random.randint(jax.random.fold_in(key, 13), (PIECES, PIECES, P_SIZE), 0, NI * CJ * (NK - 1))
    return (picked // (NK - 1) * NK + picked % (NK - 1)).astype(jnp.int32)


def draw_receptor_cell(key, part):
    total = NI * CJ * NK
    key_order, key_count, key_block, key_line = jax.random.split(jax.random.fold_in(key, 21), 4)
    orders = jax.vmap(lambda one_key: jax.random.permutation(one_key, total))(jax.random.split(key_order, PIECES))
    chosen = orders[:, :PIECES * P_SIZE].reshape(PIECES, PIECES, P_SIZE)
    counts = jax.random.randint(key_count, (PIECES, PIECES), P_SIZE // 4, P_SIZE + 1)
    receiver = jnp.arange(PIECES)
    offset = jax.random.randint(key_block, (PIECES,), 1, BLOCKS)
    full_line = jax.random.randint(key_line, (PIECES,), 0, RANGES)
    full_sender = (receiver // RANGES + offset) % BLOCKS * RANGES + full_line
    sender = jnp.arange(PIECES)
    counts = jnp.where(sender[None, :] == full_sender[:, None], P_SIZE, counts)
    counts = jnp.where(receiver[:, None] // RANGES == sender[None, :] // RANGES, 0, counts)
    slots = jnp.arange(P_SIZE)
    return jnp.where(slots[None, None, :] < counts[:, :, None], chosen, total).astype(jnp.int32)


def steps_of(rng, extent, cuts, smallest, largest):
    def one(position, parts):
        heights = jax.random.uniform(jax.random.fold_in(jax.random.fold_in(rng, 6), position), (parts,), jnp.float32, smallest / len(cuts), largest / len(cuts))
        return jnp.repeat(jnp.exp(heights), extent[position] // parts).reshape((-1,) + (1,) * (len(extent) - position - 1))

    gain = one(*cuts[0])
    for cut in cuts[1:]:
        gain = gain * one(*cut)
    return gain


def scatter_about(rng, extent, width, reach, cuts=(), kind=jnp.bfloat16):
    entries = jax.random.normal(rng, extent, jnp.float32) * width
    if len(cuts) > 0:
        entries = steps_of(rng, extent, cuts, -0.22, 0.18) * entries
    return jnp.clip(entries, min=-reach, max=reach).astype(kind)


def setup_inputs(seed: int = 0) -> dict:
    keys = jax.random.split(jax.random.key(seed), 10)
    return {
        "state": scatter_about(keys[0], (BLOCKS, VARS, NI, NJ, NK), 1.0, 6.0, ((0, 8), (3, 16)), jnp.float32),
        "first_flux": scatter_about(keys[1], (BLOCKS, VARS, VARS), 20 ** -0.5, 1.25, ((0, 8),), jnp.float32),
        "second_flux": scatter_about(keys[2], (BLOCKS, VARS, VARS), 20 ** -0.5, 1.25, ((0, 8),), jnp.float32),
        "viscosity": jnp.clip(jnp.exp(math.log(0.15) - 2.014903 * jax.random.uniform(keys[3], (BLOCKS,), jnp.float32) ** steps_of(keys[3], (BLOCKS,), ((0, 8),), -0.2, 0.2)), 0.02, 0.15),
        "first_inverse": draw_first_inverse(jax.random.fold_in(keys[9], 71), 0),
        "second_inverse": draw_second_inverse(jax.random.fold_in(keys[9], 71), 0),
        "donor_cell": draw_donor_cell(jax.random.fold_in(keys[9], 71), 0),
        "donor_weight": jnp.clip(1.0 * jax.random.uniform(keys[7], (PIECES, PIECES, P_SIZE), jnp.float32) ** steps_of(keys[7], (PIECES, PIECES, P_SIZE), ((0, 128),), -0.2, 0.2), 0.0, 1.0),
        "receptor_cell": draw_receptor_cell(jax.random.fold_in(keys[9], 71), 0),
    }


highest = lax.Precision.HIGHEST


def explicit_rhs(padded, field, across_flux, lateral_flux, damping):
    plus_i = padded[:, 2:, 1:-1, 1:-1]
    minus_i = padded[:, :-2, 1:-1, 1:-1]
    plus_j = padded[:, 1:-1, 2:, 1:-1]
    minus_j = padded[:, 1:-1, :-2, 1:-1]
    plus_k = padded[:, 1:-1, 1:-1, 2:]
    minus_k = padded[:, 1:-1, 1:-1, :-2]
    laplace = plus_i + minus_i + plus_j + minus_j + plus_k + minus_k - 6.0 * field
    convect = jnp.einsum('uv,vijk->uijk', across_flux, plus_i - minus_i, precision=highest)
    convect = convect + jnp.einsum('uv,vijk->uijk', lateral_flux, plus_j - minus_j, precision=highest)
    return damping * laplace - 0.5 * convect


def reference(state, first_flux, second_flux, viscosity, first_inverse, second_inverse, donor_cell, donor_weight, receptor_cell):
    total = NI * CJ * NK
    current = state
    for step_index in range(ITERS):
        pieces = current.reshape(BLOCKS, VARS, NI, RANGES, CJ, NK).transpose(0, 3, 1, 2, 4, 5).reshape(PIECES, VARS, total)

        def donate(local_piece, cells, weights):
            flat_cells = cells.reshape(-1).astype(jnp.int32)
            first_value = jnp.take(local_piece, flat_cells, axis=1)
            second_value = jnp.take(local_piece, flat_cells + 1, axis=1)
            flat_weight = weights.reshape(-1)
            return (flat_weight * first_value + (1.0 - flat_weight) * second_value).reshape(VARS, PIECES, P_SIZE)

        donated = jax.vmap(donate)(pieces, donor_cell, donor_weight)
        arrived = donated.transpose(2, 1, 0, 3)

        def receive(local_piece, cells, values):
            return local_piece.at[:, cells.reshape(-1).astype(jnp.int32)].set(values.reshape(VARS, -1), mode="drop")

        fringed = jax.vmap(receive)(pieces, receptor_cell, arrived)
        fringed = fringed.reshape(BLOCKS, RANGES, VARS, NI, CJ, NK).transpose(0, 2, 3, 1, 4, 5).reshape(BLOCKS, VARS, NI, NJ, NK)

        def advance_block(inputs):
            field, across_flux, lateral_flux, damping, matrix_first, matrix_second = inputs
            padded = jnp.pad(field, ((0, 0), (1, 1), (1, 1), (1, 1)))
            rhs_part = explicit_rhs(padded, field, across_flux, lateral_flux, damping)
            line_i = jnp.einsum('ab,vbjk->vajk', matrix_first, rhs_part, precision=highest)
            line_j = jnp.einsum('ab,vibk->viak', matrix_second, line_i, precision=highest)
            return field + line_j

        current = lax.map(advance_block, (fringed, first_flux, second_flux, viscosity, first_inverse, second_inverse))
    return current
```

```python
import jax
import jax.numpy as jnp
from jax import lax
from jax.experimental import pallas as pl
from jax.experimental.pallas import tpu as pltpu
from jax.sharding import PartitionSpec as P

V, NI, CJ, NK, PIECES, SLOTS, RANGES = 5, 256, 4, 128, 128, 128, 16
ROWS = NI * CJ
CHUNK = NI // RANGES
NJ = CJ * RANGES
highest = lax.Precision.HIGHEST
f32 = jnp.float32


def to_rows(st_ref, tiles):
    def one(b, carry):
        for v in range(V):
            tiles[pl.ds(b * 64 + v, 8, stride=8), :] = st_ref[pl.ds(v * ROWS + b * 8, 8), :]
        return carry

    lax.fori_loop(0, ROWS // 8, one, 0)


def tile_of(tiles, cell):
    return tiles.at[pl.ds(pl.multiple_of((cell >> 7) * 8, 8), 8), :]


def gather_kernel(cell_ref, lane_ref, weight_ref, st_ref, out_ref, tiles):
    to_rows(st_ref, tiles)
    lane = lax.broadcasted_iota(jnp.int32, (8, 128), 1)
    odd = lane & 1
    half = lane >> 1
    even = (lane * 2) & 127

    def piece(m, carry):
        cells = jnp.broadcast_to(lane_ref[pl.ds(m, 1), :] & 127, (8, 128))
        weights = jnp.broadcast_to(weight_ref[pl.ds(m, 1), :], (8, 128))
        sums = []
        for h in range(2):
            pick = half + 64 * h
            want = jnp.take_along_axis(cells, pick, axis=1) + odd
            w = jnp.take_along_axis(weights, pick, axis=1)
            w = jnp.where(odd == 0, w, 1.0 - w)
            acc = jnp.zeros((8, 128), f32)
            for q in range(64):
                x = tile_of(tiles, cell_ref[m, 64 * h + q])[...]
                acc = jnp.where(half == q, jnp.take_along_axis(x, want, axis=1), acc)
            acc = acc * w
            acc = acc + pltpu.roll(acc, 127, axis=1)
            sums.append(jnp.take_along_axis(acc, even, axis=1))
        out_ref[m] = jnp.where(lane < 64, sums[0], sums[1])[:V]
        return carry

    lax.fori_loop(0, PIECES, piece, 0)


def scatter_kernel(cell_ref, arrived_ref, st_ref, field_ref, edge_ref, tiles):
    to_rows(st_ref, tiles)
    lane = lax.broadcasted_iota(jnp.int32, (8, 128), 1)

    def piece(n, carry):
        values = jnp.concatenate([arrived_ref[n], jnp.zeros((3, 128), f32)], axis=0)
        for p in range(SLOTS):
            cell = cell_ref[n, p]
            value = jnp.broadcast_to(values[:, p : p + 1], (8, 128))
            pltpu.store(tile_of(tiles, cell), value, mask=lane == (cell & 127))
        return carry

    lax.fori_loop(0, PIECES, piece, 0)
    zero = jnp.zeros((8, 128), f32)
    for j in range(CJ):
        for v in range(V):
            field_ref[j, v, pl.ds(0, 8), :] = zero
            field_ref[j, v, pl.ds(NI + 8, 8), :] = zero

    def one(b, carry):
        for j in range(CJ):
            for v in range(V):
                x = tiles[pl.ds(b * 256 + j * 8 + v, 8, stride=32), :]
                field_ref[j, v, pl.ds(8 + b * 8, 8), :] = x
                if j in (0, CJ - 1):
                    edge_ref[j // (CJ - 1), v, pl.ds(b * 8, 8), :] = x
        return carry

    lax.fori_loop(0, NI // 8, one, 0)


def first_kernel(js, a_ref, b_ref, damp_ref, field_ref, low_ref, high_ref, inverse_ref, out_ref, rhs):
    lane = lax.broadcasted_iota(jnp.int32, (8, 128), 1)
    damp = damp_ref[0]
    a = [[0.5 * a_ref[0, u, v] for v in range(V)] for u in range(V)]
    b = [[0.5 * b_ref[0, u, v] for v in range(V)] for u in range(V)]
    for slot, j in enumerate(js):

        def one(t, carry):
            base = pl.multiple_of(t * 8, 8)
            di, dj, lap = [], [], []
            for v in range(V):
                c = field_ref[j, v, pl.ds(base + 8, 8), :]
                wide = field_ref[j, v, pl.ds(base, 24), :]
                im, ip = wide[7:15], wide[9:17]
                if j == 0:
                    jm = low_ref[v, pl.ds(base, 8), :]
                else:
                    jm = field_ref[j - 1, v, pl.ds(base + 8, 8), :]
                if j == CJ - 1:
                    jp = high_ref[v, pl.ds(base, 8), :]
                else:
                    jp = field_ref[j + 1, v, pl.ds(base + 8, 8), :]
                kp = jnp.where(lane == NK - 1, 0.0, pltpu.roll(c, NK - 1, axis=1))
                km = jnp.where(lane == 0, 0.0, pltpu.roll(c, 1, axis=1))
                lap.append(ip + im + jp + jm + kp + km - 6.0 * c)
                di.append(ip - im)
                dj.append(jp - jm)
            for u in range(V):
                r = damp * lap[u]
                for v in range(V):
                    r = r - (a[u][v] * di[v] + b[u][v] * dj[v])
                rhs[pl.ds(base, 8), pl.ds(u * NK, NK)] = r
            return carry

        lax.fori_loop(0, NI // 8, one, 0)
        solved = jnp.dot(inverse_ref[...], rhs[...], precision=highest, preferred_element_type=f32)
        for u in range(V):
            out_ref[:, u, slot] = solved[:, u * NK : (u + 1) * NK].reshape(RANGES, CHUNK, NK)


def second_kernel(inverse_ref, in_ref, out_ref, wide, solved):
    step = V * CJ * CHUNK
    for v in range(V):
        for j in range(CJ):
            for i in range(CHUNK):
                for s in range(0, RANGES, 8):
                    start = s * step + (v * CJ + j) * CHUNK + i
                    wide[j * RANGES + s : j * RANGES + s + 8, i * NK : (i + 1) * NK] = in_ref[
                        pl.ds(start, 8, stride=step), :
                    ]
        solved[...] = jnp.dot(inverse_ref[...], wide[...], precision=highest, preferred_element_type=f32)
        for j in range(CJ):
            for i in range(CHUNK):
                for s in range(0, RANGES, 8):
                    start = s * step + (v * CJ + j) * CHUNK + i
                    out_ref[pl.ds(start, 8, stride=step), :] = solved[
                        j * RANGES + s : j * RANGES + s + 8, i * NK : (i + 1) * NK
                    ]


def add_kernel(field_ref, back_ref, out_ref):
    def one(t, carry):
        for v in range(V):
            for j in range(CJ):
                for h in range(CHUNK // 8):
                    i = t * CHUNK + h * 8
                    x = field_ref[j, v, pl.ds(pl.multiple_of(i + 8, 8), 8), :] + back_ref[t, v, j, pl.ds(h * 8, 8), :]
                    out_ref[pl.ds(v * ROWS + i * CJ + j, 8, stride=CJ), :] = x
        return carry

    lax.fori_loop(0, RANGES, one, 0)


smem = pl.BlockSpec(memory_space=pltpu.SMEM)
vmem = pl.BlockSpec(memory_space=pltpu.VMEM)


def run(kernel, specs, shapes, scratch, limit, *args):
    one = not isinstance(shapes, list)
    shapes = [shapes] if one else shapes
    out = pl.pallas_call(
        kernel,
        out_shape=[jax.ShapeDtypeStruct(s, f32) for s in shapes],
        in_specs=specs,
        out_specs=[vmem] * len(shapes),
        scratch_shapes=[pltpu.VMEM(s, f32) for s in scratch],
        compiler_params=pltpu.CompilerParams(vmem_limit_bytes=limit << 20),
    )(*args)
    return out[0] if one else out


def gather_call(cells, weights, st):
    return run(gather_kernel, [smem, vmem, vmem, vmem], (PIECES, V, SLOTS), [((ROWS + 8) * 8, NK)], 16, cells, cells, weights, st)


def scatter_call(cells, arrived, st):
    return run(
        scatter_kernel,
        [smem, vmem, vmem],
        [(CJ, V, NI + 16, NK), (2, V, NI, NK)],
        [((ROWS + 8) * 8, NK)],
        20,
        cells,
        arrived,
        st,
    )


def first_call(js, a, b, damp, field, low, high, inverse):
    def kernel(*refs):
        first_kernel(js, *refs)

    return run(
        kernel,
        [smem, smem, smem, vmem, vmem, vmem, vmem],
        (RANGES, V, len(js), CHUNK, NK),
        [(NI, V * NK)],
        20,
        a,
        b,
        damp,
        field,
        low,
        high,
        inverse,
    )


def second_call(inverse, lines):
    order = inverse.reshape(RANGES, CJ, RANGES, CJ).transpose(1, 0, 3, 2).reshape(NJ, NJ)
    rows = RANGES * V * CJ * CHUNK
    return run(
        second_kernel,
        [vmem, vmem],
        (rows, NK),
        [(NJ, CHUNK * NK), (NJ, CHUNK * NK)],
        20,
        order,
        lines.reshape(rows, NK),
    ).reshape(RANGES, V, CJ, CHUNK, NK)


def add_call(field, back):
    return run(add_kernel, [vmem, vmem], (V * ROWS, NK), [], 20, field, back)


def body(
    state,
    first_flux,
    second_flux,
    viscosity,
    first_inverse,
    second_inverse,
    donor_cell,
    donor_weight,
    receptor_cell,
):
    st = state.reshape(V * ROWS, NK)
    donated = gather_call(donor_cell[0], donor_weight[0], st)
    arrived = lax.all_to_all(donated, ("blk", "line"), split_axis=0, concat_axis=0, tiled=True)
    field, edges = scatter_call(receptor_cell[0], arrived, st)
    up = [(i, i + 1) for i in range(RANGES - 1)]
    down = [(i + 1, i) for i in range(RANGES - 1)]
    low = lax.ppermute(edges[1], "line", up)
    high = lax.ppermute(edges[0], "line", down)
    lines = first_call(
        range(CJ), first_flux, second_flux, viscosity, field, low, high, first_inverse[0]
    )
    lines = lax.all_to_all(lines, "line", split_axis=0, concat_axis=0, tiled=True)
    back = second_call(second_inverse[0], lines)
    back = lax.all_to_all(back, "line", split_axis=0, concat_axis=0, tiled=True)
    out = add_call(field, back)
    return out.reshape(1, V, NI, CJ, NK)


def solution(mesh):
    in_specs = (
        P("blk", None, None, "line", None),
        P("blk", None, None),
        P("blk", None, None),
        P("blk"),
        P("blk", None, None),
        P("blk", None, None),
        P(("blk", "line"), None, None),
        P(("blk", "line"), None, None),
        P(("blk", "line"), None, None),
    )
    out_specs = P("blk", None, None, "line", None)
    return jax.shard_map(body, mesh=mesh, in_specs=in_specs, out_specs=out_specs, check_vma=False)
```

```python
import jax
import jax.numpy as jnp
from jax import lax
from jax.experimental import pallas as pl
from jax.experimental.pallas import tpu as pltpu
from jax.sharding import PartitionSpec as P

V, NI, CJ, NK, PIECES, SLOTS, RANGES = 5, 256, 4, 128, 128, 128, 16
ROWS = NI * CJ
CHUNK = NI // RANGES
NJ = CJ * RANGES
highest = lax.Precision.HIGHEST
f32 = jnp.float32


def to_rows(st_ref, tiles):
    def one(b, carry):
        for v in range(V):
            tiles[pl.ds(b * 64 + v, 8, stride=8), :] = st_ref[pl.ds(v * ROWS + b * 8, 8), :]
        return carry

    lax.fori_loop(0, ROWS // 8, one, 0)


def tile_of(tiles, cell):
    return tiles.at[pl.ds(pl.multiple_of((cell >> 7) * 8, 8), 8), :]


def gather_kernel(cell_ref, lane_ref, weight_ref, st_ref, out_ref, tiles, want, mix, picked):
    to_rows(st_ref, tiles)
    lane = lax.broadcasted_iota(jnp.int32, (8, 128), 1)
    sub = lax.broadcasted_iota(jnp.int32, (8, 128), 0)
    odd = lane & 1
    half = lane >> 1
    even = (lane * 2) & 127

    def before(b, carry):
        for t in range(4):
            r = pl.ds(pl.multiple_of(b * 32 + t * 8, 8), 8)
            cells = lane_ref[r, :] & 127
            weights = weight_ref[r, :]
            for h in range(2):
                want[h, r, :] = jnp.take_along_axis(cells, half + 64 * h, axis=1) + odd
                w = jnp.take_along_axis(weights, half + 64 * h, axis=1)
                mix[h, r, :] = jnp.where(odd == 0, w, 1.0 - w)
        return carry

    lax.fori_loop(0, PIECES // 32, before, 0)

    def piece(m, carry):
        for h in range(2):
            index = jnp.broadcast_to(want[h, pl.ds(m, 1), :], (8, 128))
            acc = jnp.zeros((8, 128), f32)
            for q in range(64):
                x = tile_of(tiles, cell_ref[m, 64 * h + q])[...]
                acc = jnp.where(half == q, jnp.take_along_axis(x, index, axis=1), acc)
            picked[m, h] = acc * jnp.broadcast_to(mix[h, pl.ds(m, 1), :], (8, 128))
        return carry

    lax.fori_loop(0, PIECES, piece, 0, unroll=4)

    def after(b, carry):
        for t in range(8):
            sums = []
            for h in range(2):
                x = picked[b * 8 + t, h]
                x = x + pltpu.roll(x, 127, axis=1)
                sums.append(jnp.take_along_axis(x, even, axis=1))
            x = jnp.where(lane < 64, sums[0], sums[1])
            out_ref[b * 8 + t] = jnp.where(sub < V, x, 0.0)
        return carry

    lax.fori_loop(0, PIECES // 8, after, 0)


def scatter_kernel(offset_ref, cell_ref, arrived_ref, st_ref, field_ref, low_ref, high_ref, tiles, parts, ping, pong):
    to_rows(st_ref, tiles)
    sub = lax.broadcasted_iota(jnp.int32, (8, 128), 0)

    def build(b, carry):
        r = pl.ds(pl.multiple_of(b * 16, 16), 16)
        x = []
        for t in range(2):
            lanes = (cell_ref[pl.ds(2 * b + t, 1), :] & 127).astype(f32)
            values = arrived_ref[pl.ds(pl.multiple_of(b * 16 + t * 8, 8), 8), :]
            x.append(jnp.where(sub == V, jnp.broadcast_to(lanes, (8, 128)), values))
        x = jnp.concatenate(x, axis=0)
        coarse = x.astype(jnp.bfloat16)
        parts[r, 0:128] = coarse
        parts[r, 128:256] = (x - coarse.astype(f32)).astype(jnp.bfloat16)
        return carry

    lax.fori_loop(0, PIECES // 2, build, 0, unroll=4)
    lane = lax.broadcasted_iota(jnp.int32, (8, 128), 1).astype(f32)
    square = (2 * SLOTS, 2 * NK)
    code = (lax.broadcasted_iota(jnp.int32, square, 0) & 127) - (lax.broadcasted_iota(jnp.int32, square, 1) >> 7)

    def spread(pair, buffer):
        ones = jnp.where(code == 2 * pair, 1.0, 0.0).astype(jnp.bfloat16)
        buffer[...] = jnp.dot(parts[...], ones, preferred_element_type=f32)

    def put(pair, buffer):
        for c in range(2):
            columns = slice(c * 128, c * 128 + 128)
            for n in range(PIECES):
                offset = pl.multiple_of(offset_ref[2 * pair + c, n], 8)
                value = buffer[n * 8 : n * 8 + 8, columns]
                lanes = jnp.broadcast_to(buffer[n * 8 + V : n * 8 + V + 1, columns], (8, 128))
                pltpu.store(tiles.at[pl.ds(offset, 8), :], value, mask=lane == lanes)

    spread(0, ping)

    def both(i, carry):
        spread(2 * i + 1, pong)
        put(2 * i, ping)
        spread(2 * i + 2, ping)
        put(2 * i + 1, pong)
        return carry

    lax.fori_loop(0, SLOTS // 4, both, 0)
    zero = jnp.zeros((8, 128), f32)
    for j in range(CJ):
        for v in range(V):
            field_ref[j, v, pl.ds(0, 8), :] = zero
            field_ref[j, v, pl.ds(NI + 8, 8), :] = zero

    def one(b, carry):
        for j in range(CJ):
            for v in range(V):
                x = tiles[pl.ds(b * 256 + j * 8 + v, 8, stride=32), :]
                field_ref[j, v, pl.ds(pl.multiple_of(8 + b * 8, 8), 8), :] = x
                if j == 0:
                    low_ref[v, pl.ds(pl.multiple_of(b * 8, 8), 8), :] = x
                if j == CJ - 1:
                    high_ref[v, pl.ds(pl.multiple_of(b * 8, 8), 8), :] = x
        return carry

    lax.fori_loop(0, NI // 8, one, 0)


def first_kernel(js, a_ref, b_ref, damp_ref, field_ref, inverse_ref, low_ref, high_ref, out_ref, coarse, fine):
    rows = 16
    lane = lax.broadcasted_iota(jnp.int32, (rows, 128), 1)
    damp = damp_ref[0]
    a = [[0.5 * a_ref[0, u, v] for v in range(V)] for u in range(V)]
    b = [[0.5 * b_ref[0, u, v] for v in range(V)] for u in range(V)]
    matrix = inverse_ref[...]
    matrix_coarse = matrix.astype(jnp.bfloat16)
    matrix_fine = (matrix - matrix_coarse.astype(f32)).astype(jnp.bfloat16)

    def dot(x, y):
        return jnp.dot(x, y, preferred_element_type=f32)

    for slot, j in enumerate(js):

        def one(t, carry):
            base = pl.multiple_of(t * rows, rows)
            di, dj, lap = [], [], []
            for v in range(V):
                c = field_ref[j, v, pl.ds(base + 8, rows), :]
                im = field_ref[j, v, pl.ds(base + 7, rows), :]
                ip = field_ref[j, v, pl.ds(base + 9, rows), :]
                if j == 0:
                    jm = low_ref[v, pl.ds(base, rows), :]
                else:
                    jm = field_ref[j - 1, v, pl.ds(base + 8, rows), :]
                if j == CJ - 1:
                    jp = high_ref[v, pl.ds(base, rows), :]
                else:
                    jp = field_ref[j + 1, v, pl.ds(base + 8, rows), :]
                kp = jnp.where(lane == NK - 1, 0.0, pltpu.roll(c, NK - 1, axis=1))
                km = jnp.where(lane == 0, 0.0, pltpu.roll(c, 1, axis=1))
                lap.append(ip + im + jp + jm + kp + km - 6.0 * c)
                di.append(ip - im)
                dj.append(jp - jm)
            for u in range(V):
                r = damp * lap[u]
                for v in range(V):
                    r = r - (a[u][v] * di[v] + b[u][v] * dj[v])
                big = r.astype(jnp.bfloat16)
                coarse[slot, pl.ds(base, rows), pl.ds(u * NK, NK)] = big
                fine[slot, pl.ds(base, rows), pl.ds(u * NK, NK)] = (r - big.astype(f32)).astype(jnp.bfloat16)
            return carry

        lax.fori_loop(0, NI // rows, one, 0)
        x, y = coarse[slot], fine[slot]
        solved = dot(matrix_coarse, x) + (dot(matrix_coarse, y) + dot(matrix_fine, x))
        for u in range(V):
            out_ref[:, u, slot] = solved[:, u * NK : (u + 1) * NK].reshape(RANGES, CHUNK, NK)


def second_kernel(inverse_ref, middle_ref, edge_ref, out_ref, wide, solved):
    step = V * CJ * CHUNK
    half = V * 2 * CHUNK
    places = [(edge_ref, 0), (middle_ref, 0), (middle_ref, 1), (edge_ref, 1)]
    for v in range(V):
        for j in range(CJ):
            ref, slot = places[j]
            for i in range(CHUNK):
                for s in range(0, RANGES, 8):
                    start = s * half + (v * 2 + slot) * CHUNK + i
                    wide[j * RANGES + s : j * RANGES + s + 8, i * NK : (i + 1) * NK] = ref[
                        pl.ds(start, 8, stride=half), :
                    ]
        solved[...] = jnp.dot(inverse_ref[...], wide[...], precision=highest, preferred_element_type=f32)
        for j in range(CJ):
            for i in range(CHUNK):
                for s in range(0, RANGES, 8):
                    start = s * step + (v * CJ + j) * CHUNK + i
                    out_ref[pl.ds(start, 8, stride=step), :] = solved[
                        j * RANGES + s : j * RANGES + s + 8, i * NK : (i + 1) * NK
                    ]


def add_kernel(field_ref, back_ref, out_ref):
    def one(t, carry):
        for v in range(V):
            for j in range(CJ):
                for h in range(CHUNK // 8):
                    i = t * CHUNK + h * 8
                    x = field_ref[j, v, pl.ds(pl.multiple_of(i + 8, 8), 8), :] + back_ref[t, v, j, pl.ds(h * 8, 8), :]
                    out_ref[pl.ds(v * ROWS + i * CJ + j, 8, stride=CJ), :] = x
        return carry

    lax.fori_loop(0, RANGES, one, 0)


smem = pl.BlockSpec(memory_space=pltpu.SMEM)
vmem = pl.BlockSpec(memory_space=pltpu.VMEM)


def run(kernel, specs, shapes, scratch, limit, moved, *args):
    one = not isinstance(shapes, list)
    shapes = [shapes] if one else shapes
    out = pl.pallas_call(
        kernel,
        out_shape=[jax.ShapeDtypeStruct(s, f32) for s in shapes],
        in_specs=specs,
        out_specs=[vmem] * len(shapes),
        scratch_shapes=[pltpu.VMEM(s, t) for s, t in scratch],
        compiler_params=pltpu.CompilerParams(vmem_limit_bytes=limit << 20),
        cost_estimate=pl.CostEstimate(flops=0, bytes_accessed=moved << 20, transcendentals=0),
    )(*args)
    return out[0] if one else out


TILES = (((ROWS + 8) * 8, NK), f32)


def gather_call(cells, weights, st):
    scratch = [TILES, ((2, PIECES, NK), jnp.int32), ((2, PIECES, NK), f32), ((PIECES, 2, 8, NK), f32)]
    return run(gather_kernel, [smem, vmem, vmem, vmem], (PIECES, 8, SLOTS), scratch, 16, 90, cells, cells, weights, st)


def scatter_call(cells, arrived, st):
    offsets = ((cells >> 7) * 8).T
    wide = (PIECES * 8, 2 * NK)
    return run(
        scatter_kernel,
        [smem, vmem, vmem, vmem],
        [(CJ, V, NI + 16, NK), (V, NI, NK), (V, NI, NK)],
        [TILES, (wide, jnp.bfloat16), (wide, f32), (wide, f32)],
        24,
        100,
        offsets,
        cells,
        arrived.reshape(PIECES * 8, NK),
        st,
    )


def first_call(js, a, b, damp, field, inverse, *layers):
    def middle_kernel(a_ref, b_ref, damp_ref, field_ref, inverse_ref, out_ref, coarse, fine):
        first_kernel(js, a_ref, b_ref, damp_ref, field_ref, inverse_ref, None, None, out_ref, coarse, fine)

    def edge_kernel(*refs):
        first_kernel(js, *refs)

    pair = ((len(js), NI, V * NK), jnp.bfloat16)
    return run(
        edge_kernel if layers else middle_kernel,
        [smem, smem, smem] + [vmem] * (2 + len(layers)),
        (RANGES, V, len(js), CHUNK, NK),
        [pair, pair],
        16,
        20,
        a,
        b,
        damp,
        field,
        inverse,
        *layers,
    )


def second_call(inverse, middle, edge):
    order = inverse.reshape(RANGES, CJ, RANGES, CJ).transpose(1, 0, 3, 2).reshape(NJ, NJ)
    rows = RANGES * V * CJ * CHUNK
    wide = ((NJ, CHUNK * NK), f32)
    return run(
        second_kernel,
        [vmem, vmem, vmem],
        (rows, NK),
        [wide, wide],
        16,
        20,
        order,
        middle.reshape(rows // 2, NK),
        edge.reshape(rows // 2, NK),
    ).reshape(RANGES, V, CJ, CHUNK, NK)


def add_call(field, back):
    return run(add_kernel, [vmem, vmem], (V * ROWS, NK), [], 16, 7, field, back)


def exchange(x, axes):
    return lax.all_to_all(x, axes, split_axis=0, concat_axis=0, tiled=True)


def body(
    state,
    first_flux,
    second_flux,
    viscosity,
    first_inverse,
    second_inverse,
    donor_cell,
    donor_weight,
    receptor_cell,
):
    st = state.reshape(V * ROWS, NK)
    donated = gather_call(donor_cell[0], donor_weight[0], st)
    arrived = exchange(donated, ("blk", "line"))
    field, first_layer, last_layer = scatter_call(receptor_cell[0], arrived, st)
    low = lax.ppermute(last_layer, "line", [(i, i + 1) for i in range(RANGES - 1)])
    high = lax.ppermute(first_layer, "line", [(i + 1, i) for i in range(RANGES - 1)])
    shared = (first_flux, second_flux, viscosity, field, first_inverse[0])
    middle = exchange(first_call((1, 2), *shared), "line")
    edge = exchange(first_call((0, 3), *shared, low, high), "line")
    back = exchange(second_call(second_inverse[0], middle, edge), "line")
    return add_call(field, back).reshape(1, V, NI, CJ, NK)


def solution(mesh):
    in_specs = (
        P("blk", None, None, "line", None),
        P("blk", None, None),
        P("blk", None, None),
        P("blk"),
        P("blk", None, None),
        P("blk", None, None),
        P(("blk", "line"), None, None),
        P(("blk", "line"), None, None),
        P(("blk", "line"), None, None),
    )
    out_specs = P("blk", None, None, "line", None)
    return jax.shard_map(body, mesh=mesh, in_specs=in_specs, out_specs=out_specs, check_vma=False)
```

```python
import jax
import jax.numpy as jnp
from jax import lax
from jax.experimental import pallas as pl
from jax.experimental.pallas import tpu as pltpu
from jax.sharding import PartitionSpec as P

V, NI, CJ, NK, PIECES, SLOTS, RANGES = 5, 256, 4, 128, 128, 128, 16
ROWS = NI * CJ
DEPTH = (ROWS + 8) * 8
CHUNK = NI // RANGES
NJ = CJ * RANGES
highest = lax.Precision.HIGHEST
f32 = jnp.float32


def gather_kernel(offset_ref, lane_ref, weight_ref, st_ref, out_ref, kept_ref, tiles, want, mix, picked, sem):
    lane = lax.broadcasted_iota(jnp.int32, (8, 128), 1)
    sub = lax.broadcasted_iota(jnp.int32, (8, 128), 0)
    odd = lane & 1
    half = lane >> 1
    even = (lane * 2) & 127
    def lay(b, carry):
        for t in range(2):
            c = b * 2 + t
            for v in range(V):
                tiles[pl.ds(c * 64 + v, 8, stride=8), :] = st_ref[
                    pl.ds(pl.multiple_of(v * ROWS + c * 8, 8), 8), :
                ]
        return carry

    lax.fori_loop(0, ROWS // 16, lay, 0)
    keep = pltpu.make_async_copy(tiles, kept_ref, sem)
    keep.start()

    def before(b, carry):
        for t in range(4):
            r = pl.ds(pl.multiple_of(b * 32 + t * 8, 8), 8)
            cells = lane_ref[r, :] & 127
            weights = weight_ref[r, :]
            for h in range(2):
                want[h, r, :] = jnp.take_along_axis(cells, half + 64 * h, axis=1) + odd
                w = jnp.take_along_axis(weights, half + 64 * h, axis=1)
                mix[h, r, :] = jnp.where(odd == 0, w, 1.0 - w)
        return carry

    lax.fori_loop(0, PIECES // 32, before, 0)

    def piece(m, carry):
        for h in range(2):
            index = jnp.broadcast_to(want[h, pl.ds(m, 1), :], (8, 128))
            acc = jnp.zeros((8, 128), f32)
            for q in range(64):
                x = tiles[pl.ds(pl.multiple_of(offset_ref[m, 64 * h + q], 8), 8), :]
                acc = jnp.where(half == q, jnp.take_along_axis(x, index, axis=1), acc)
            picked[m, h] = acc * jnp.broadcast_to(mix[h, pl.ds(m, 1), :], (8, 128))
        return carry

    lax.fori_loop(0, PIECES, piece, 0, unroll=8)

    def after(b, carry):
        for t in range(16):
            sums = []
            for h in range(2):
                x = picked[b * 16 + t, h]
                x = x + pltpu.roll(x, 127, axis=1)
                sums.append(jnp.take_along_axis(x, even, axis=1))
            x = jnp.where(lane < 64, sums[0], sums[1])
            out_ref[b * 16 + t] = jnp.where(sub < V, x, 0.0)
        return carry

    lax.fori_loop(0, PIECES // 16, after, 0)
    keep.wait()


def scatter_kernel(offset_ref, cell_ref, arrived_ref, kept_ref, field_ref, low_ref, high_ref, tiles, parts, ping, pong, sem):
    keep = pltpu.make_async_copy(kept_ref, tiles, sem)
    keep.start()
    sub = lax.broadcasted_iota(jnp.int32, (8, 128), 0)

    def build(b, carry):
        r = pl.ds(pl.multiple_of(b * 16, 16), 16)
        x = []
        for t in range(2):
            lanes = (cell_ref[pl.ds(2 * b + t, 1), :] & 127).astype(f32)
            values = arrived_ref[pl.ds(pl.multiple_of(b * 16 + t * 8, 8), 8), :]
            x.append(jnp.where(sub == V, jnp.broadcast_to(lanes, (8, 128)), values))
        x = jnp.concatenate(x, axis=0)
        coarse = x.astype(jnp.bfloat16)
        parts[r, 0:128] = coarse
        parts[r, 128:256] = (x - coarse.astype(f32)).astype(jnp.bfloat16)
        return carry

    lax.fori_loop(0, PIECES // 2, build, 0, unroll=4)
    lane = lax.broadcasted_iota(jnp.int32, (8, 128), 1).astype(f32)
    square = (2 * SLOTS, 2 * NK)
    code = (lax.broadcasted_iota(jnp.int32, square, 0) & 127) - (lax.broadcasted_iota(jnp.int32, square, 1) >> 7)
    group = PIECES // 4

    def ones(pair):
        return jnp.where(code == 2 * pair, 1.0, 0.0).astype(jnp.bfloat16)

    def spread(mask, buffer, g):
        rows = slice(g * group * 8, (g + 1) * group * 8)
        buffer[rows, :] = jnp.dot(parts[rows, :], mask, preferred_element_type=f32)

    def put(pair, buffer, g):
        for n in range(g * group, (g + 1) * group):
            for c in range(2):
                columns = slice(c * 128, c * 128 + 128)
                offset = pl.multiple_of(offset_ref[2 * pair + c, n], 8)
                value = buffer[n * 8 : n * 8 + 8, columns]
                lanes = jnp.broadcast_to(buffer[n * 8 + V : n * 8 + V + 1, columns], (8, 128))
                pltpu.store(tiles.at[pl.ds(offset, 8), :], value, mask=lane == lanes)

    def step(pair, now, later):
        mask = ones(pair + 1)
        for g in range(4):
            spread(mask, later, g)
            put(pair, now, g)

    first = ones(0)
    for g in range(4):
        spread(first, ping, g)
    keep.wait()

    def both(i, carry):
        step(2 * i, ping, pong)
        step(2 * i + 1, pong, ping)
        return carry

    lax.fori_loop(0, SLOTS // 4, both, 0)
    zero = jnp.zeros((8, 128), f32)
    for j in range(CJ):
        for v in range(V):
            field_ref[j, v, pl.ds(0, 8), :] = zero
            field_ref[j, v, pl.ds(NI + 8, 8), :] = zero

    def one(b, carry):
        for j in range(CJ):
            for v in range(V):
                x = tiles[pl.ds(b * 256 + j * 8 + v, 8, stride=32), :]
                field_ref[j, v, pl.ds(pl.multiple_of(8 + b * 8, 8), 8), :] = x
                if j == 0:
                    low_ref[v, pl.ds(pl.multiple_of(b * 8, 8), 8), :] = x
                if j == CJ - 1:
                    high_ref[v, pl.ds(pl.multiple_of(b * 8, 8), 8), :] = x
        return carry

    lax.fori_loop(0, NI // 8, one, 0)


def first_kernel(js, a_ref, b_ref, damp_ref, field_ref, inverse_ref, low_ref, high_ref, put, coarse, fine):
    rows = 16
    lane = lax.broadcasted_iota(jnp.int32, (rows, 128), 1)
    damp = damp_ref[0]
    a = [[0.5 * a_ref[0, u, v] for v in range(V)] for u in range(V)]
    b = [[0.5 * b_ref[0, u, v] for v in range(V)] for u in range(V)]
    matrix = inverse_ref[...]
    matrix_coarse = matrix.astype(jnp.bfloat16)
    matrix_fine = (matrix - matrix_coarse.astype(f32)).astype(jnp.bfloat16)

    def dot(x, y):
        return jnp.dot(x, y, preferred_element_type=f32)

    for slot, j in enumerate(js):

        def one(t, carry):
            base = pl.multiple_of(t * rows, rows)

            def cells(v, di, j):
                return field_ref[j, v, pl.ds(base + 8 + di, rows), :]

            di, dj, lap = [], [], []
            for v in range(V):
                c = cells(v, 0, j)
                im = cells(v, -1, j)
                ip = cells(v, 1, j)
                jm = low_ref[v, pl.ds(base, rows), :] if j == 0 else cells(v, 0, j - 1)
                jp = high_ref[v, pl.ds(base, rows), :] if j == CJ - 1 else cells(v, 0, j + 1)
                kp = jnp.where(lane == NK - 1, 0.0, pltpu.roll(c, NK - 1, axis=1))
                km = jnp.where(lane == 0, 0.0, pltpu.roll(c, 1, axis=1))
                lap.append(ip + im + jp + jm + kp + km - 6.0 * c)
                di.append(ip - im)
                dj.append(jp - jm)
            for u in range(V):
                r = damp * lap[u]
                for v in range(V):
                    r = r - (a[u][v] * di[v] + b[u][v] * dj[v])
                big = r.astype(jnp.bfloat16)
                coarse[slot, pl.ds(base, rows), pl.ds(u * NK, NK)] = big
                fine[slot, pl.ds(base, rows), pl.ds(u * NK, NK)] = (r - big.astype(f32)).astype(jnp.bfloat16)
            return carry

        lax.fori_loop(0, NI // rows, one, 0)
        x, y = coarse[slot], fine[slot]
        solved = dot(matrix_coarse, x) + (dot(matrix_coarse, y) + dot(matrix_fine, x))
        for u in range(V):
            put(u, slot, j, solved[:, u * NK : (u + 1) * NK].reshape(RANGES, CHUNK, NK))


def middle_kernel(a_ref, b_ref, damp_ref, field_ref, inverse_ref, out_ref, coarse, fine):
    def put(u, slot, j, value):
        out_ref[:, u, slot] = value

    first_kernel((1, 2), a_ref, b_ref, damp_ref, field_ref, inverse_ref, None, None, put, coarse, fine)


def edge_kernel(a_ref, b_ref, damp_ref, field_ref, inverse_ref, low_ref, high_ref, middle_ref, out_ref, coarse, fine):
    def put(u, slot, j, value):
        out_ref[:, u, j] = value

    for u in range(V):
        out_ref[:, u, 1:3] = middle_ref[:, u]
    first_kernel((0, 3), a_ref, b_ref, damp_ref, field_ref, inverse_ref, low_ref, high_ref, put, coarse, fine)


def second_kernel(inverse_ref, in_ref, out_ref, wide, solved):
    step = V * CJ * CHUNK
    for v in range(V):
        for j in range(CJ):
            for i in range(CHUNK):
                for s in range(0, RANGES, 8):
                    start = s * step + (v * CJ + j) * CHUNK + i
                    wide[j * RANGES + s : j * RANGES + s + 8, i * NK : (i + 1) * NK] = in_ref[
                        pl.ds(start, 8, stride=step), :
                    ]
        solved[...] = jnp.dot(inverse_ref[...], wide[...], precision=highest, preferred_element_type=f32)
        for j in range(CJ):
            for i in range(CHUNK):
                for s in range(0, RANGES, 8):
                    start = s * step + (v * CJ + j) * CHUNK + i
                    out_ref[pl.ds(start, 8, stride=step), :] = solved[
                        j * RANGES + s : j * RANGES + s + 8, i * NK : (i + 1) * NK
                    ]


def add_kernel(field_ref, back_ref, out_ref):
    def one(t, carry):
        for v in range(V):
            for j in range(CJ):
                for h in range(CHUNK // 8):
                    i = t * CHUNK + h * 8
                    x = field_ref[j, v, pl.ds(pl.multiple_of(i + 8, 8), 8), :] + back_ref[t, v, j, pl.ds(h * 8, 8), :]
                    out_ref[pl.ds(v * ROWS + i * CJ + j, 8, stride=CJ), :] = x
        return carry

    lax.fori_loop(0, RANGES, one, 0)


smem = pl.BlockSpec(memory_space=pltpu.SMEM)
vmem = pl.BlockSpec(memory_space=pltpu.VMEM)
hbm = pl.BlockSpec(memory_space=pltpu.HBM)


def run(kernel, specs, shapes, scratch, limit, *args, outs=None, sems=0):
    one = not isinstance(shapes, list)
    shapes = [shapes] if one else shapes
    out = pl.pallas_call(
        kernel,
        out_shape=[jax.ShapeDtypeStruct(s, f32) for s in shapes],
        in_specs=specs,
        out_specs=outs or [vmem] * len(shapes),
        scratch_shapes=[pltpu.VMEM(s, t) for s, t in scratch] + [pltpu.SemaphoreType.DMA] * sems,
        compiler_params=pltpu.CompilerParams(vmem_limit_bytes=limit << 20),
    )(*args)
    return out[0] if one else out


def offsets_of(cells):
    return (cells >> 7) * 8


def gather_call(cells, weights, st):
    scratch = [((DEPTH, NK), f32), ((2, PIECES, NK), jnp.int32), ((2, PIECES, NK), f32), ((PIECES, 2, 8, NK), f32)]
    shapes = [(PIECES, 8, SLOTS), (DEPTH, NK)]
    specs = [smem, vmem, vmem, vmem]
    args = (offsets_of(cells), cells, weights, st)
    return run(gather_kernel, specs, shapes, scratch, 48, *args, outs=[vmem, hbm], sems=1)


def scatter_call(cells, arrived, kept):
    wide = (PIECES * 8, 2 * NK)
    return run(
        scatter_kernel,
        [smem, vmem, vmem, hbm],
        [(CJ, V, NI + 16, NK), (V, NI, NK), (V, NI, NK)],
        [((DEPTH, NK), f32), (wide, jnp.bfloat16), (wide, f32), (wide, f32)],
        48,
        offsets_of(cells).T,
        cells,
        arrived.reshape(PIECES * 8, NK),
        kept,
        sems=1,
    )


def middle_call(*shared):
    pair = ((2, NI, V * NK), jnp.bfloat16)
    return run(middle_kernel, [smem] * 3 + [vmem] * 2, (RANGES, V, 2, CHUNK, NK), [pair, pair], 20, *shared)


def edge_call(*shared):
    pair = ((2, NI, V * NK), jnp.bfloat16)
    return run(edge_kernel, [smem] * 3 + [vmem] * 5, (RANGES, V, CJ, CHUNK, NK), [pair, pair], 20, *shared)


def ordered(inverse):
    return inverse.reshape(RANGES, CJ, RANGES, CJ).transpose(1, 0, 3, 2).reshape(NJ, NJ)


def second_call(order, lines):
    rows = RANGES * V * CJ * CHUNK
    wide = ((NJ, CHUNK * NK), f32)
    out = run(second_kernel, [vmem, vmem], (rows, NK), [wide, wide], 20, order, lines.reshape(rows, NK))
    return out.reshape(RANGES, V, CJ, CHUNK, NK)


def add_call(field, back):
    return run(add_kernel, [vmem, vmem], (V * ROWS, NK), [], 20, field, back)


def exchange(x, axes):
    return lax.all_to_all(x, axes, split_axis=0, concat_axis=0, tiled=True)


def body(
    state,
    first_flux,
    second_flux,
    viscosity,
    first_inverse,
    second_inverse,
    donor_cell,
    donor_weight,
    receptor_cell,
):
    st = state.reshape(V * ROWS, NK)
    donated, kept = gather_call(donor_cell[0], donor_weight[0], st)
    arrived = exchange(donated, ("blk", "line"))
    field, first_layer, last_layer = scatter_call(receptor_cell[0], arrived, kept)
    low = lax.ppermute(last_layer, "line", [(i, i + 1) for i in range(RANGES - 1)])
    high = lax.ppermute(first_layer, "line", [(i + 1, i) for i in range(RANGES - 1)])
    shared = (first_flux, second_flux, viscosity, field, first_inverse[0])
    middle = middle_call(*shared)
    order = ordered(second_inverse[0])
    lines, order = lax.optimization_barrier((edge_call(*shared, low, high, middle), order))
    lines = exchange(lines, "line")
    back = exchange(second_call(order, lines), "line")
    return add_call(field, back).reshape(1, V, NI, CJ, NK)


def solution(mesh):
    in_specs = (
        P("blk", None, None, "line", None),
        P("blk", None, None),
        P("blk", None, None),
        P("blk"),
        P("blk", None, None),
        P("blk", None, None),
        P(("blk", "line"), None, None),
        P(("blk", "line"), None, None),
        P(("blk", "line"), None, None),
    )
    out_specs = P("blk", None, None, "line", None)
    return jax.shard_map(body, mesh=mesh, in_specs=in_specs, out_specs=out_specs, check_vma=False)
```

```python
import jax
import jax.numpy as jnp
from jax import lax
from jax.experimental import pallas as pl
from jax.experimental.pallas import tpu as pltpu
from jax.sharding import PartitionSpec as P

V, NI, CJ, NK, PIECES, SLOTS, RANGES = 5, 256, 4, 128, 128, 128, 16
ROWS = NI * CJ
PAD = CJ
DEPTH = (ROWS + 2 * PAD) * 8
CHUNK = NI // RANGES
SLAB = (CHUNK + 2) * CJ
NJ = CJ * RANGES
f32 = jnp.float32


def gather_kernel(offset_ref, lane_ref, weight_ref, st_ref, out_ref, kept_ref, tiles, want, mix, picked, sem):
    lane = lax.broadcasted_iota(jnp.int32, (8, 128), 1)
    sub = lax.broadcasted_iota(jnp.int32, (8, 128), 0)
    odd = lane & 1
    half = lane >> 1
    even = (lane * 2) & 127
    for t in range(PAD):
        tiles[t * 8 : t * 8 + 8, :] = jnp.zeros((8, 128), f32)

    def lay(b, carry):
        for t in range(2):
            c = b * 2 + t
            for v in range(V):
                tiles[pl.ds(PAD * 8 + c * 64 + v, 8, stride=8), :] = st_ref[
                    pl.ds(pl.multiple_of(v * ROWS + c * 8, 8), 8), :
                ]
        return carry

    lax.fori_loop(0, ROWS // 16, lay, 0)
    keep = pltpu.make_async_copy(tiles, kept_ref, sem)
    keep.start()

    def before(b, carry):
        for t in range(4):
            r = pl.ds(pl.multiple_of(b * 32 + t * 8, 8), 8)
            cells = lane_ref[r, :] & 127
            weights = weight_ref[r, :]
            for h in range(2):
                want[h, r, :] = jnp.take_along_axis(cells, half + 64 * h, axis=1) + odd
                w = jnp.take_along_axis(weights, half + 64 * h, axis=1)
                mix[h, r, :] = jnp.where(odd == 0, w, 1.0 - w)
        return carry

    lax.fori_loop(0, PIECES // 32, before, 0)

    def piece(m, carry):
        for h in range(2):
            index = jnp.broadcast_to(want[h, pl.ds(m, 1), :], (8, 128))
            acc = jnp.zeros((8, 128), f32)
            for q in range(64):
                x = tiles[pl.ds(pl.multiple_of(offset_ref[m, 64 * h + q], 8), 8), :]
                acc = jnp.where(half == q, jnp.take_along_axis(x, index, axis=1), acc)
            picked[m, h] = acc * jnp.broadcast_to(mix[h, pl.ds(m, 1), :], (8, 128))
        return carry

    lax.fori_loop(0, PIECES, piece, 0, unroll=8)

    def after(b, carry):
        for t in range(16):
            sums = []
            for h in range(2):
                x = picked[b * 16 + t, h]
                x = x + pltpu.roll(x, 127, axis=1)
                sums.append(jnp.take_along_axis(x, even, axis=1))
            x = jnp.where(lane < 64, sums[0], sums[1])
            out_ref[b * 16 + t] = jnp.where(sub < V, x, 0.0)
        return carry

    lax.fori_loop(0, PIECES // 16, after, 0)
    keep.wait()


def scatter_kernel(offset_ref, cell_ref, arrived_ref, kept_ref, send_ref, tiles, parts, ping, pong, sem):
    keep = pltpu.make_async_copy(kept_ref, tiles, sem)
    keep.start()
    sub = lax.broadcasted_iota(jnp.int32, (8, 128), 0)

    def build(b, carry):
        r = pl.ds(pl.multiple_of(b * 16, 16), 16)
        x = []
        for t in range(2):
            lanes = (cell_ref[pl.ds(2 * b + t, 1), :] & 127).astype(f32)
            values = arrived_ref[pl.ds(pl.multiple_of(b * 16 + t * 8, 8), 8), :]
            x.append(jnp.where(sub == V, jnp.broadcast_to(lanes, (8, 128)), values))
        x = jnp.concatenate(x, axis=0)
        coarse = x.astype(jnp.bfloat16)
        parts[r, 0:128] = coarse
        parts[r, 128:256] = (x - coarse.astype(f32)).astype(jnp.bfloat16)
        return carry

    lax.fori_loop(0, PIECES // 2, build, 0, unroll=4)
    lane = lax.broadcasted_iota(jnp.int32, (8, 128), 1).astype(f32)
    square = (2 * SLOTS, 2 * NK)
    code = (lax.broadcasted_iota(jnp.int32, square, 0) & 127) - (lax.broadcasted_iota(jnp.int32, square, 1) >> 7)
    group = PIECES // 4

    def ones(pair):
        return jnp.where(code == 2 * pair, 1.0, 0.0).astype(jnp.bfloat16)

    def spread(mask, buffer, g):
        rows = slice(g * group * 8, (g + 1) * group * 8)
        buffer[rows, :] = jnp.dot(parts[rows, :], mask, preferred_element_type=f32)

    def put(pair, buffer, g):
        for n in range(g * group, (g + 1) * group):
            for c in range(2):
                columns = slice(c * 128, c * 128 + 128)
                offset = pl.multiple_of(offset_ref[2 * pair + c, n], 8)
                value = buffer[n * 8 : n * 8 + 8, columns]
                lanes = jnp.broadcast_to(buffer[n * 8 + V : n * 8 + V + 1, columns], (8, 128))
                pltpu.store(tiles.at[pl.ds(offset, 8), :], value, mask=lane == lanes)

    def step(pair, now, later):
        mask = ones(pair + 1)
        for g in range(4):
            spread(mask, later, g)
            put(pair, now, g)

    first = ones(0)
    for g in range(4):
        spread(first, ping, g)
    keep.wait()

    def both(i, carry):
        step(2 * i, ping, pong)
        step(2 * i + 1, pong, ping)
        return carry

    lax.fori_loop(0, SLOTS // 4, both, 0)
    for t in range(PAD):
        tiles[(PAD + ROWS + t) * 8 : (PAD + ROWS + t + 1) * 8, :] = jnp.zeros((8, 128), f32)

    def slab(c, carry):
        for v in range(V):
            for t in range(0, SLAB, 8):
                send_ref[pl.ds(pl.multiple_of((c * V + v) * SLAB + t, 8), 8), :] = tiles[
                    pl.ds((c * CHUNK * CJ + t) * 8 + v, 8, stride=8), :
                ]
        return carry

    lax.fori_loop(0, RANGES, slab, 0)


def halves(x):
    coarse = x.astype(jnp.bfloat16)
    return coarse, (x - coarse.astype(f32)).astype(jnp.bfloat16)


def product(x, y):
    def dot(p, q):
        return jnp.dot(p, q, preferred_element_type=f32)

    return dot(x[0], y[0]) + (dot(x[0], y[1]) + dot(x[1], y[0]))


def slab_kernel(a_ref, b_ref, damp_ref, inverse_ref, in_ref, out_ref, rhs, coarse, fine):
    lane = lax.broadcasted_iota(jnp.int32, (CHUNK, 128), 1)
    damp = damp_ref[0]
    a = [[0.5 * a_ref[0, u, v] for v in range(V)] for u in range(V)]
    b = [[0.5 * b_ref[0, u, v] for v in range(V)] for u in range(V)]

    def one(s, carry):
        def cells(s, v, di, j):
            return in_ref[pl.ds((s * V + v) * SLAB + (1 + di) * CJ + j, CHUNK, stride=CJ), :]

        for j in range(CJ):
            di, dj, lap = [], [], []
            for v in range(V):
                c = cells(s, v, 0, j)
                im = cells(s, v, -1, j)
                ip = cells(s, v, 1, j)
                if j == 0:
                    jm = jnp.where(s > 0, cells(jnp.maximum(s - 1, 0), v, 0, CJ - 1), 0.0)
                else:
                    jm = cells(s, v, 0, j - 1)
                if j == CJ - 1:
                    jp = jnp.where(s < RANGES - 1, cells(jnp.minimum(s + 1, RANGES - 1), v, 0, 0), 0.0)
                else:
                    jp = cells(s, v, 0, j + 1)
                kp = jnp.where(lane == NK - 1, 0.0, pltpu.roll(c, NK - 1, axis=1))
                km = jnp.where(lane == 0, 0.0, pltpu.roll(c, 1, axis=1))
                lap.append(ip + im + jp + jm + kp + km - 6.0 * c)
                di.append(ip - im)
                dj.append(jp - jm)
            for u in range(V):
                r = damp * lap[u]
                for v in range(V):
                    r = r - (a[u][v] * di[v] + b[u][v] * dj[v])
                rhs[u, pl.ds(pl.multiple_of((s * CJ + j) * CHUNK, CHUNK), CHUNK), :] = r
        return carry

    lax.fori_loop(0, RANGES, one, 0)
    matrix = halves(jnp.concatenate([inverse_ref[pl.ds(j, RANGES, stride=CJ), :] for j in range(CJ)], axis=0))
    step = V * CJ * CHUNK
    for u in range(V):
        for i in range(CHUNK):
            columns = slice(i * NK, (i + 1) * NK)
            coarse[:, columns], fine[:, columns] = halves(rhs[u, pl.ds(i, NJ, stride=CHUNK), :])
        solved = product(matrix, (coarse[...], fine[...]))
        for j in range(CJ):
            for i in range(CHUNK):
                for s in range(0, RANGES, 8):
                    start = s * step + (u * CJ + j) * CHUNK + i
                    out_ref[pl.ds(start, 8, stride=step), :] = solved[
                        j * RANGES + s : j * RANGES + s + 8, i * NK : (i + 1) * NK
                    ]


def final_kernel(inverse_ref, send_ref, back_ref, out_ref):
    matrix = halves(inverse_ref[...])
    for v in range(V):
        lines = jnp.concatenate([back_ref[:, v, j].reshape(NI, NK) for j in range(CJ)], axis=1)
        solved = product(matrix, halves(lines))
        for j in range(CJ):
            for c in range(RANGES):
                x = send_ref[pl.ds((c * V + v) * SLAB + CJ + j, CHUNK, stride=CJ), :]
                out_ref[pl.ds(v * ROWS + c * CHUNK * CJ + j, CHUNK, stride=CJ), :] = (
                    x + solved[c * CHUNK : (c + 1) * CHUNK, j * NK : (j + 1) * NK]
                )


smem = pl.BlockSpec(memory_space=pltpu.SMEM)
vmem = pl.BlockSpec(memory_space=pltpu.VMEM)
hbm = pl.BlockSpec(memory_space=pltpu.HBM)


def run(kernel, specs, shapes, scratch, limit, *args, outs=None, sems=0):
    one = not isinstance(shapes, list)
    shapes = [shapes] if one else shapes
    out = pl.pallas_call(
        kernel,
        out_shape=[jax.ShapeDtypeStruct(s, f32) for s in shapes],
        in_specs=specs,
        out_specs=outs or [vmem] * len(shapes),
        scratch_shapes=[pltpu.VMEM(s, t) for s, t in scratch] + [pltpu.SemaphoreType.DMA] * sems,
        compiler_params=pltpu.CompilerParams(vmem_limit_bytes=limit << 20),
    )(*args)
    return out[0] if one else out


def offsets_of(cells):
    return ((cells >> 7) + PAD) * 8


def gather_call(cells, weights, st):
    scratch = [((DEPTH, NK), f32), ((2, PIECES, NK), jnp.int32), ((2, PIECES, NK), f32), ((PIECES, 2, 8, NK), f32)]
    shapes = [(PIECES, 8, SLOTS), (DEPTH, NK)]
    specs = [smem, vmem, vmem, vmem]
    args = (offsets_of(cells), cells, weights, st)
    return run(gather_kernel, specs, shapes, scratch, 48, *args, outs=[vmem, hbm], sems=1)


def scatter_call(cells, arrived, kept):
    wide = (PIECES * 8, 2 * NK)
    return run(
        scatter_kernel,
        [smem, vmem, vmem, hbm],
        (RANGES * V * SLAB, NK),
        [((DEPTH, NK), f32), (wide, jnp.bfloat16), (wide, f32), (wide, f32)],
        48,
        offsets_of(cells).T,
        cells,
        arrived.reshape(PIECES * 8, NK),
        kept,
        sems=1,
    )


def slab_call(a, b, damp, inverse, lines):
    wide = ((NJ, CHUNK * NK), jnp.bfloat16)
    return run(
        slab_kernel,
        [smem, smem, smem, vmem, vmem],
        (RANGES * V * CJ * CHUNK, NK),
        [((V, NJ * CHUNK, NK), f32), wide, wide],
        20,
        a,
        b,
        damp,
        inverse,
        lines,
    )


def final_call(inverse, send, back):
    back = back.reshape(RANGES, V, CJ, CHUNK, NK)
    return run(final_kernel, [vmem] * 3, (V * ROWS, NK), [], 20, inverse, send, back)


def exchange(x, axes):
    return lax.all_to_all(x, axes, split_axis=0, concat_axis=0, tiled=True)


def body(
    state,
    first_flux,
    second_flux,
    viscosity,
    first_inverse,
    second_inverse,
    donor_cell,
    donor_weight,
    receptor_cell,
):
    st = state.reshape(V * ROWS, NK)
    donated, kept = gather_call(donor_cell[0], donor_weight[0], st)
    arrived = exchange(donated, ("blk", "line"))
    send = scatter_call(receptor_cell[0], arrived, kept)
    lines = exchange(send, "line")
    back = exchange(slab_call(first_flux, second_flux, viscosity, second_inverse[0], lines), "line")
    return final_call(first_inverse[0], send, back).reshape(1, V, NI, CJ, NK)


def solution(mesh):
    in_specs = (
        P("blk", None, None, "line", None),
        P("blk", None, None),
        P("blk", None, None),
        P("blk"),
        P("blk", None, None),
        P("blk", None, None),
        P(("blk", "line"), None, None),
        P(("blk", "line"), None, None),
        P(("blk", "line"), None, None),
    )
    out_specs = P("blk", None, None, "line", None)
    return jax.shard_map(body, mesh=mesh, in_specs=in_specs, out_specs=out_specs, check_vma=False)
```

```python
import jax
import jax.numpy as jnp
from jax import lax
from jax.experimental import pallas as pl
from jax.experimental.pallas import tpu as pltpu
from jax.sharding import PartitionSpec as P

V, NI, CJ, NK, PIECES, SLOTS, RANGES = 5, 256, 4, 128, 128, 128, 16
ROWS = NI * CJ
PAD = CJ
DEPTH = (ROWS + 2 * PAD) * 8
CHUNK = NI // RANGES
SLAB = (CHUNK + 2) * CJ
NJ = CJ * RANGES
f32 = jnp.float32


def others(block, n):
    return n + jnp.where(n >= block * RANGES, RANGES, 0)


def gather_kernel(cell_hbm, weight_hbm, st_hbm, out_ref, kept_ref, lane_ref, weight_ref, st_ref, offset_vmem, tiles, want, mix, picked, offset_ref, sems):
    copies = [
        pltpu.make_async_copy(cell_hbm, lane_ref, sems.at[0]),
        pltpu.make_async_copy(weight_hbm, weight_ref, sems.at[1]),
        pltpu.make_async_copy(st_hbm, st_ref, sems.at[2]),
    ]
    for copy in copies:
        copy.start()
    block = lax.axis_index("blk")
    lane = lax.broadcasted_iota(jnp.int32, (8, 128), 1)
    sub = lax.broadcasted_iota(jnp.int32, (8, 128), 0)
    odd = lane & 1
    half = lane >> 1
    even = (lane * 2) & 127
    copies[0].wait()
    offset_vmem[...] = ((lane_ref[...] >> 7) + PAD) * 8
    offsets = pltpu.make_async_copy(offset_vmem, offset_ref, sems.at[0])
    offsets.start()
    copies[1].wait()

    def before(b, carry):
        for t in range(4):
            r = pl.ds(pl.multiple_of(b * 32 + t * 8, 8), 8)
            cells = lane_ref[r, :] & 127
            weights = weight_ref[r, :]
            for h in range(2):
                want[h, r, :] = jnp.take_along_axis(cells, half + 64 * h, axis=1) + odd
                w = jnp.take_along_axis(weights, half + 64 * h, axis=1)
                mix[h, r, :] = jnp.where(odd == 0, w, 1.0 - w)
        return carry

    lax.fori_loop(0, PIECES // 32, before, 0)

    copies[2].wait()
    for t in range(PAD):
        tiles[t * 8 : t * 8 + 8, :] = jnp.zeros((8, 128), f32)
        tiles[DEPTH - t * 8 - 8 : DEPTH - t * 8, :] = jnp.zeros((8, 128), f32)

    def lay(b, carry):
        for t in range(2):
            c = b * 2 + t
            for v in range(V):
                tiles[pl.ds(PAD * 8 + c * 64 + v, 8, stride=8), :] = st_ref[
                    pl.ds(pl.multiple_of(v * ROWS + c * 8, 8), 8), :
                ]
        return carry

    lax.fori_loop(0, ROWS // 16, lay, 0)
    keep = pltpu.make_async_copy(tiles, kept_ref, sems.at[2])
    keep.start()
    offsets.wait()

    def own(m, carry):
        for h in range(2):
            picked[block * RANGES + m, h] = jnp.zeros((8, 128), f32)
        return carry

    lax.fori_loop(0, RANGES, own, 0)

    def piece(k, carry):
        m = others(block, k)
        for h in range(2):
            index = jnp.broadcast_to(want[h, pl.ds(m, 1), :], (8, 128))
            acc = jnp.zeros((8, 128), f32)
            for q in range(64):
                x = tiles[pl.ds(pl.multiple_of(offset_ref[m, 64 * h + q], 8), 8), :]
                acc = jnp.where(half == q, jnp.take_along_axis(x, index, axis=1), acc)
            picked[m, h] = acc * jnp.broadcast_to(mix[h, pl.ds(m, 1), :], (8, 128))
        return carry

    lax.fori_loop(0, PIECES - RANGES, piece, 0, unroll=8)

    def after(b, carry):
        for t in range(16):
            sums = []
            for h in range(2):
                x = picked[b * 16 + t, h]
                x = x + pltpu.roll(x, 127, axis=1)
                sums.append(jnp.take_along_axis(x, even, axis=1))
            x = jnp.where(lane < 64, sums[0], sums[1])
            for v in range(V):
                out_ref[b * 16 + t, :, v * SLOTS : (v + 1) * SLOTS] = x[v : v + 1]
        return carry

    lax.fori_loop(0, PIECES // 16, after, 0)
    keep.wait()


def scatter_kernel(offset_ref, a_ref, b_ref, damp_ref, cell_ref, arrived_ref, kept_ref, send_ref, factor_ref, tiles, parts, ping, pong, sem):
    block = lax.axis_index("blk")
    keep = pltpu.make_async_copy(kept_ref, tiles, sem)
    keep.start()
    sub = lax.broadcasted_iota(jnp.int32, (8, 128), 0)

    def build(b, carry):
        r = pl.ds(pl.multiple_of(b * 16, 16), 16)
        x = []
        for t in range(2):
            n = others(block, 2 * b + t)
            lanes = (cell_ref[pl.ds(n, 1), :] & 127).astype(f32)
            values = jnp.broadcast_to(lanes, (8, 128))
            for v in range(V):
                row = arrived_ref[n, :, v * SLOTS : (v + 1) * SLOTS]
                values = jnp.where(sub == v, jnp.broadcast_to(row, (8, 128)), values)
            x.append(values)
        x = jnp.concatenate(x, axis=0)
        coarse = x.astype(jnp.bfloat16)
        parts[r, 0:128] = coarse
        parts[r, 128:256] = (x - coarse.astype(f32)).astype(jnp.bfloat16)
        return carry

    lax.fori_loop(0, (PIECES - RANGES) // 2, build, 0, unroll=4)
    for u in range(V):
        for v in range(V):
            factor_ref[u * V + v : u * V + v + 1, :] = jnp.full((1, 128), 0.5 * a_ref[0, u, v], f32)
            factor_ref[25 + u * V + v : 26 + u * V + v, :] = jnp.full((1, 128), 0.5 * b_ref[0, u, v], f32)
    factor_ref[50:51, :] = jnp.full((1, 128), damp_ref[0], f32)
    factor_ref[51:56, :] = jnp.zeros((5, 128), f32)
    lane = lax.broadcasted_iota(jnp.int32, (8, 128), 1).astype(f32)
    square = (2 * SLOTS, 2 * NK)
    code = (lax.broadcasted_iota(jnp.int32, square, 0) & 127) - (lax.broadcasted_iota(jnp.int32, square, 1) >> 7)
    group = (PIECES - RANGES) // 4

    def ones(pair):
        return jnp.where(code == 2 * pair, 1.0, 0.0).astype(jnp.bfloat16)

    def spread(mask, buffer, g):
        rows = slice(g * group * 8, (g + 1) * group * 8)
        buffer[rows, :] = jnp.dot(parts[rows, :], mask, preferred_element_type=f32)

    def put(pair, buffer, g):
        for n in range(g * group, (g + 1) * group):
            for c in range(2):
                columns = slice(c * 128, c * 128 + 128)
                offset = pl.multiple_of(offset_ref[2 * pair + c, n], 8)
                value = buffer[n * 8 : n * 8 + 8, columns]
                lanes = jnp.broadcast_to(buffer[n * 8 + V : n * 8 + V + 1, columns], (8, 128))
                pltpu.store(tiles.at[pl.ds(offset, 8), :], value, mask=lane == lanes)

    def step(pair, now, later):
        mask = ones(pair + 1)
        for g in range(4):
            spread(mask, later, g)
            put(pair, now, g)

    first = ones(0)
    for g in range(4):
        spread(first, ping, g)
    keep.wait()

    def both(i, carry):
        step(2 * i, ping, pong)
        step(2 * i + 1, pong, ping)
        return carry

    lax.fori_loop(0, SLOTS // 4, both, 0)
    for t in range(PAD):
        tiles[(PAD + ROWS + t) * 8 : (PAD + ROWS + t + 1) * 8, :] = jnp.zeros((8, 128), f32)

    def slab(c, carry):
        for v in range(V):
            for t in range(0, SLAB, 8):
                send_ref[pl.ds(pl.multiple_of((c * V + v) * SLAB + t, 8), 8), :] = tiles[
                    pl.ds((c * CHUNK * CJ + t) * 8 + v, 8, stride=8), :
                ]
        return carry

    lax.fori_loop(0, RANGES, slab, 0)


def halves(x):
    coarse = x.astype(jnp.bfloat16)
    return coarse, (x - coarse.astype(f32)).astype(jnp.bfloat16)


def product(x, y):
    def dot(p, q):
        return jnp.dot(p, q, preferred_element_type=f32)

    return dot(x[0], y[0]) + (dot(x[0], y[1]) + dot(x[1], y[0]))


def slab_kernel(factor_ref, inverse_ref, in_ref, out_ref, rhs, coarse, fine):
    lane = lax.broadcasted_iota(jnp.int32, (CHUNK, 128), 1)

    def factor(r):
        return jnp.broadcast_to(factor_ref[r : r + 1, :], (CHUNK, 128))

    def one(s, carry):
        def cells(s, v, di, j):
            return in_ref[pl.ds((s * V + v) * SLAB + (1 + di) * CJ + j, CHUNK, stride=CJ), :]

        for j in range(CJ):
            di, dj, lap = [], [], []
            for v in range(V):
                c = cells(s, v, 0, j)
                im = cells(s, v, -1, j)
                ip = cells(s, v, 1, j)
                if j == 0:
                    jm = jnp.where(s > 0, cells(jnp.maximum(s - 1, 0), v, 0, CJ - 1), 0.0)
                else:
                    jm = cells(s, v, 0, j - 1)
                if j == CJ - 1:
                    jp = jnp.where(s < RANGES - 1, cells(jnp.minimum(s + 1, RANGES - 1), v, 0, 0), 0.0)
                else:
                    jp = cells(s, v, 0, j + 1)
                kp = jnp.where(lane == NK - 1, 0.0, pltpu.roll(c, NK - 1, axis=1))
                km = jnp.where(lane == 0, 0.0, pltpu.roll(c, 1, axis=1))
                lap.append(ip + im + jp + jm + kp + km - 6.0 * c)
                di.append(ip - im)
                dj.append(jp - jm)
            for u in range(V):
                r = factor(50) * lap[u]
                for v in range(V):
                    r = r - (factor(u * V + v) * di[v] + factor(25 + u * V + v) * dj[v])
                rhs[u, pl.ds(pl.multiple_of((s * CJ + j) * CHUNK, CHUNK), CHUNK), :] = r
        return carry

    lax.fori_loop(0, RANGES, one, 0)
    matrix = halves(jnp.concatenate([inverse_ref[pl.ds(j, RANGES, stride=CJ), :] for j in range(CJ)], axis=0))
    step = V * CJ * CHUNK
    for u in range(V):
        for i in range(CHUNK):
            columns = slice(i * NK, (i + 1) * NK)
            coarse[:, columns], fine[:, columns] = halves(rhs[u, pl.ds(i, NJ, stride=CHUNK), :])
        solved = product(matrix, (coarse[...], fine[...]))
        for j in range(CJ):
            for i in range(CHUNK):
                for s in range(0, RANGES, 8):
                    start = s * step + (u * CJ + j) * CHUNK + i
                    out_ref[pl.ds(start, 8, stride=step), :] = solved[
                        j * RANGES + s : j * RANGES + s + 8, i * NK : (i + 1) * NK
                    ]


def final_kernel(inverse_ref, send_hbm, back_ref, out_hbm, send_ref, out_ref, sems):
    bring = pltpu.make_async_copy(send_hbm, send_ref, sems.at[V])
    bring.start()
    matrix = halves(inverse_ref[...])
    copies = []
    for v in range(V):
        lines = jnp.concatenate([back_ref[:, v, j].reshape(NI, NK) for j in range(CJ)], axis=1)
        solved = product(matrix, halves(lines))
        if v == 0:
            bring.wait()
        for j in range(CJ):
            for c in range(RANGES):
                x = send_ref[pl.ds((c * V + v) * SLAB + CJ + j, CHUNK, stride=CJ), :]
                out_ref[pl.ds(v * ROWS + c * CHUNK * CJ + j, CHUNK, stride=CJ), :] = (
                    x + solved[c * CHUNK : (c + 1) * CHUNK, j * NK : (j + 1) * NK]
                )
        rows = pl.ds(v * ROWS, ROWS)
        copies.append(pltpu.make_async_copy(out_ref.at[rows, :], out_hbm.at[rows, :], sems.at[v]))
        copies[-1].start()
    for copy in copies:
        copy.wait()


smem = pl.BlockSpec(memory_space=pltpu.SMEM)
vmem = pl.BlockSpec(memory_space=pltpu.VMEM)
hbm = pl.BlockSpec(memory_space=pltpu.HBM)


def run(kernel, specs, shapes, scratch, limit, *args, outs=None, more=None):
    one = not isinstance(shapes, list)
    shapes = [shapes] if one else shapes
    out = pl.pallas_call(
        kernel,
        out_shape=[jax.ShapeDtypeStruct(s, f32) for s in shapes],
        in_specs=specs,
        out_specs=outs or [vmem] * len(shapes),
        scratch_shapes=[pltpu.VMEM(s, t) for s, t in scratch] + (more or []),
        compiler_params=pltpu.CompilerParams(vmem_limit_bytes=limit << 20),
    )(*args)
    return out[0] if one else out


LANES = ((PIECES, SLOTS), jnp.int32)


def gather_call(cells, weights, st):
    scratch = [LANES, ((PIECES, SLOTS), f32), ((V * ROWS, NK), f32), LANES, ((DEPTH, NK), f32)]
    scratch += [((2, PIECES, NK), jnp.int32), ((2, PIECES, NK), f32), ((PIECES, 2, 8, NK), f32)]
    more = [pltpu.SMEM((PIECES, SLOTS), jnp.int32), pltpu.SemaphoreType.DMA((3,))]
    shapes = [(PIECES, 1, V * SLOTS), (DEPTH, NK)]
    return run(gather_kernel, [hbm] * 3, shapes, scratch, 48, cells, weights, st, outs=[vmem, hbm], more=more)


def scatter_call(block, a, b, damp, cells, arrived, kept):
    count = PIECES - RANGES
    first = lax.broadcasted_iota(jnp.int32, (count, 1), 0) < block * RANGES
    offsets = (((jnp.where(first, cells[:count], cells[RANGES:]) >> 7) + PAD) * 8).T
    wide = (count * 8, 2 * NK)
    return run(
        scatter_kernel,
        [smem, smem, smem, smem, vmem, vmem, hbm],
        [(RANGES * V * SLAB, NK), (56, NK)],
        [((DEPTH, NK), f32), (wide, jnp.bfloat16), (wide, f32), (wide, f32)],
        48,
        offsets,
        a,
        b,
        damp,
        cells,
        arrived,
        kept,
        more=[pltpu.SemaphoreType.DMA],
    )


def slab_call(factors, inverse, lines):
    wide = ((NJ, CHUNK * NK), jnp.bfloat16)
    scratch = [((V, NJ * CHUNK, NK), f32), wide, wide]
    return run(slab_kernel, [vmem] * 3, (RANGES * V * CJ * CHUNK, NK), scratch, 20, factors, inverse, lines)


def final_call(inverse, send, back):
    back = back.reshape(RANGES, V, CJ, CHUNK, NK)
    scratch = [((RANGES * V * SLAB, NK), f32), ((V * ROWS, NK), f32)]
    more = [pltpu.SemaphoreType.DMA((V + 1,))]
    return run(final_kernel, [vmem, hbm, vmem], [(V * ROWS, NK)], scratch, 48, inverse, send, back, outs=[hbm], more=more)[0]


def exchange(x, axes):
    return lax.all_to_all(x, axes, split_axis=0, concat_axis=0, tiled=True)


def body(
    state,
    first_flux,
    second_flux,
    viscosity,
    first_inverse,
    second_inverse,
    donor_cell,
    donor_weight,
    receptor_cell,
):
    st = state.reshape(V * ROWS, NK)
    donated, kept = gather_call(donor_cell[0], donor_weight[0], st)
    arrived = exchange(donated, ("blk", "line"))
    block = lax.axis_index("blk")
    send, factors = scatter_call(block, first_flux, second_flux, viscosity, receptor_cell[0], arrived, kept)
    lines = exchange(send, "line")
    back = exchange(slab_call(factors, second_inverse[0], lines), "line")
    return final_call(first_inverse[0], send, back).reshape(1, V, NI, CJ, NK)


def solution(mesh):
    in_specs = (
        P("blk", None, None, "line", None),
        P("blk", None, None),
        P("blk", None, None),
        P("blk"),
        P("blk", None, None),
        P("blk", None, None),
        P(("blk", "line"), None, None),
        P(("blk", "line"), None, None),
        P(("blk", "line"), None, None),
    )
    out_specs = P("blk", None, None, "line", None)
    return jax.shard_map(body, mesh=mesh, in_specs=in_specs, out_specs=out_specs, check_vma=False)
```

```python
import jax
import jax.numpy as jnp
from jax import lax
from jax.experimental import pallas as pl
from jax.experimental.pallas import tpu as pltpu
from jax.sharding import PartitionSpec as P

V, NI, CJ, NK, PIECES, SLOTS, RANGES = 5, 256, 4, 128, 128, 128, 16
ROWS = NI * CJ
PAD = CJ
DEPTH = (ROWS + 2 * PAD) * 8
CHUNK = NI // RANGES
SLAB = (CHUNK + 2) * CJ
NJ = CJ * RANGES
f32 = jnp.float32


def others(block, n):
    return n + jnp.where(n >= block * RANGES, RANGES, 0)


def gather_kernel(cell_hbm, weight_hbm, st_hbm, out_ref, kept_ref, lane_ref, weight_ref, st_ref, offset_vmem, tiles, want, mix, picked, offset_ref, sems):
    copies = [
        pltpu.make_async_copy(cell_hbm, lane_ref, sems.at[0]),
        pltpu.make_async_copy(weight_hbm, weight_ref, sems.at[1]),
    ]
    for v in range(V):
        rows = pl.ds(v * ROWS, ROWS)
        copies.append(pltpu.make_async_copy(st_hbm.at[rows, :], st_ref.at[rows, :], sems.at[2 + v]))
    for copy in copies:
        copy.start()
    block = lax.axis_index("blk")
    lane = lax.broadcasted_iota(jnp.int32, (8, 128), 1)
    sub = lax.broadcasted_iota(jnp.int32, (8, 128), 0)
    odd = lane & 1
    half = lane >> 1
    even = (lane * 2) & 127
    copies[0].wait()
    offset_vmem[...] = ((lane_ref[...] >> 7) + PAD) * 8
    offsets = pltpu.make_async_copy(offset_vmem, offset_ref, sems.at[0])
    offsets.start()
    copies[1].wait()

    def before(b, carry):
        for t in range(4):
            r = pl.ds(pl.multiple_of(b * 32 + t * 8, 8), 8)
            cells = lane_ref[r, :] & 127
            weights = weight_ref[r, :]
            for h in range(2):
                want[h, r, :] = jnp.take_along_axis(cells, half + 64 * h, axis=1) + odd
                w = jnp.take_along_axis(weights, half + 64 * h, axis=1)
                mix[h, r, :] = jnp.where(odd == 0, w, 1.0 - w)
        return carry

    lax.fori_loop(0, PIECES // 32, before, 0)

    for t in range(PAD):
        tiles[t * 8 : t * 8 + 8, :] = jnp.zeros((8, 128), f32)
        tiles[DEPTH - t * 8 - 8 : DEPTH - t * 8, :] = jnp.zeros((8, 128), f32)
    for v in range(V):
        copies[2 + v].wait()

        def lay(b, carry):
            for t in range(8):
                c = b * 8 + t
                tiles[pl.ds(PAD * 8 + c * 64 + v, 8, stride=8), :] = st_ref[
                    pl.ds(pl.multiple_of(v * ROWS + c * 8, 8), 8), :
                ]
            return carry

        lax.fori_loop(0, ROWS // 64, lay, 0)
    keep = pltpu.make_async_copy(tiles, kept_ref, sems.at[2])
    keep.start()
    offsets.wait()

    def own(m, carry):
        for h in range(2):
            picked[block * RANGES + m, h] = jnp.zeros((8, 128), f32)
        return carry

    lax.fori_loop(0, RANGES, own, 0)

    def piece(k, carry):
        m = others(block, k)
        for h in range(2):
            index = jnp.broadcast_to(want[h, pl.ds(m, 1), :], (8, 128))
            acc = jnp.zeros((8, 128), f32)
            for q in range(64):
                x = tiles[pl.ds(pl.multiple_of(offset_ref[m, 64 * h + q], 8), 8), :]
                acc = jnp.where(half == q, jnp.take_along_axis(x, index, axis=1), acc)
            picked[m, h] = acc * jnp.broadcast_to(mix[h, pl.ds(m, 1), :], (8, 128))
        return carry

    lax.fori_loop(0, PIECES - RANGES, piece, 0, unroll=16)

    def after(b, carry):
        for t in range(16):
            sums = []
            for h in range(2):
                x = picked[b * 16 + t, h]
                x = x + pltpu.roll(x, 127, axis=1)
                sums.append(jnp.take_along_axis(x, even, axis=1))
            x = jnp.where(lane < 64, sums[0], sums[1])
            for v in range(V):
                out_ref[b * 16 + t, :, v * SLOTS : (v + 1) * SLOTS] = x[v : v + 1]
        return carry

    lax.fori_loop(0, PIECES // 16, after, 0)
    keep.wait()


def scatter_kernel(offset_ref, a_ref, b_ref, damp_ref, cell_ref, arrived_ref, kept_ref, send_ref, factor_ref, tiles, parts, ping, pong, sem):
    block = lax.axis_index("blk")
    keep = pltpu.make_async_copy(kept_ref, tiles, sem)
    keep.start()
    sub = lax.broadcasted_iota(jnp.int32, (8, 128), 0)

    def build(b, carry):
        r = pl.ds(pl.multiple_of(b * 16, 16), 16)
        x = []
        for t in range(2):
            n = others(block, 2 * b + t)
            lanes = (cell_ref[pl.ds(n, 1), :] & 127).astype(f32)
            values = jnp.broadcast_to(lanes, (8, 128))
            for v in range(V):
                row = arrived_ref[n, :, v * SLOTS : (v + 1) * SLOTS]
                values = jnp.where(sub == v, jnp.broadcast_to(row, (8, 128)), values)
            x.append(values)
        x = jnp.concatenate(x, axis=0)
        coarse = x.astype(jnp.bfloat16)
        parts[r, 0:128] = coarse
        parts[r, 128:256] = (x - coarse.astype(f32)).astype(jnp.bfloat16)
        return carry

    lax.fori_loop(0, (PIECES - RANGES) // 2, build, 0, unroll=4)
    for u in range(V):
        for v in range(V):
            factor_ref[u * V + v : u * V + v + 1, :] = jnp.full((1, 128), 0.5 * a_ref[0, u, v], f32)
            factor_ref[25 + u * V + v : 26 + u * V + v, :] = jnp.full((1, 128), 0.5 * b_ref[0, u, v], f32)
    factor_ref[50:51, :] = jnp.full((1, 128), damp_ref[0], f32)
    factor_ref[51:56, :] = jnp.zeros((5, 128), f32)
    lane = lax.broadcasted_iota(jnp.int32, (8, 128), 1).astype(f32)
    square = (2 * SLOTS, 2 * NK)
    code = (lax.broadcasted_iota(jnp.int32, square, 0) & 127) - (lax.broadcasted_iota(jnp.int32, square, 1) >> 7)
    group = (PIECES - RANGES) // 4

    def ones(pair):
        return jnp.where(code == 2 * pair, 1.0, 0.0).astype(jnp.bfloat16)

    def spread(mask, buffer, g):
        rows = slice(g * group * 8, (g + 1) * group * 8)
        buffer[rows, :] = jnp.dot(parts[rows, :], mask, preferred_element_type=f32)

    def put(pair, buffer, g):
        for n in range(g * group, (g + 1) * group):
            for c in range(2):
                columns = slice(c * 128, c * 128 + 128)
                offset = pl.multiple_of(offset_ref[2 * pair + c, n], 8)
                value = buffer[n * 8 : n * 8 + 8, columns]
                lanes = jnp.broadcast_to(buffer[n * 8 + V : n * 8 + V + 1, columns], (8, 128))
                pltpu.store(tiles.at[pl.ds(offset, 8), :], value, mask=lane == lanes)

    def step(pair, now, later):
        mask = ones(pair + 1)
        for g in range(4):
            spread(mask, later, g)
            put(pair, now, g)

    first = ones(0)
    for g in range(4):
        spread(first, ping, g)
    keep.wait()

    def both(i, carry):
        step(2 * i, ping, pong)
        step(2 * i + 1, pong, ping)
        return carry

    lax.fori_loop(0, SLOTS // 4, both, 0)
    for t in range(PAD):
        tiles[(PAD + ROWS + t) * 8 : (PAD + ROWS + t + 1) * 8, :] = jnp.zeros((8, 128), f32)

    def slab(c, carry):
        for v in range(V):
            for t in range(0, SLAB, 8):
                send_ref[pl.ds(pl.multiple_of((c * V + v) * SLAB + t, 8), 8), :] = tiles[
                    pl.ds((c * CHUNK * CJ + t) * 8 + v, 8, stride=8), :
                ]
        return carry

    lax.fori_loop(0, RANGES, slab, 0)


def halves(x):
    coarse = x.astype(jnp.bfloat16)
    return coarse, (x - coarse.astype(f32)).astype(jnp.bfloat16)


def product(x, y):
    def dot(p, q):
        return jnp.dot(p, q, preferred_element_type=f32)

    return dot(x[0], y[0]) + (dot(x[0], y[1]) + dot(x[1], y[0]))


def slab_kernel(factor_ref, inverse_ref, in_ref, out_ref, rhs, coarse, fine):
    lane = lax.broadcasted_iota(jnp.int32, (CHUNK, 128), 1)

    def factor(r):
        return jnp.broadcast_to(factor_ref[r : r + 1, :], (CHUNK, 128))

    def one(s, carry):
        def cells(s, v, di, j):
            return in_ref[pl.ds((s * V + v) * SLAB + (1 + di) * CJ + j, CHUNK, stride=CJ), :]

        for j in range(CJ):
            di, dj, lap = [], [], []
            for v in range(V):
                c = cells(s, v, 0, j)
                im = cells(s, v, -1, j)
                ip = cells(s, v, 1, j)
                if j == 0:
                    jm = jnp.where(s > 0, cells(jnp.maximum(s - 1, 0), v, 0, CJ - 1), 0.0)
                else:
                    jm = cells(s, v, 0, j - 1)
                if j == CJ - 1:
                    jp = jnp.where(s < RANGES - 1, cells(jnp.minimum(s + 1, RANGES - 1), v, 0, 0), 0.0)
                else:
                    jp = cells(s, v, 0, j + 1)
                kp = jnp.where(lane == NK - 1, 0.0, pltpu.roll(c, NK - 1, axis=1))
                km = jnp.where(lane == 0, 0.0, pltpu.roll(c, 1, axis=1))
                lap.append(ip + im + jp + jm + kp + km - 6.0 * c)
                di.append(ip - im)
                dj.append(jp - jm)
            for u in range(V):
                r = factor(50) * lap[u]
                for v in range(V):
                    r = r - (factor(u * V + v) * di[v] + factor(25 + u * V + v) * dj[v])
                rhs[u, pl.ds(pl.multiple_of((s * CJ + j) * CHUNK, CHUNK), CHUNK), :] = r
        return carry

    lax.fori_loop(0, RANGES, one, 0)
    matrix = halves(jnp.concatenate([inverse_ref[pl.ds(j, RANGES, stride=CJ), :] for j in range(CJ)], axis=0))
    step = V * CJ * CHUNK
    for u in range(V):
        for i in range(CHUNK):
            columns = slice(i * NK, (i + 1) * NK)
            coarse[:, columns], fine[:, columns] = halves(rhs[u, pl.ds(i, NJ, stride=CHUNK), :])
        solved = product(matrix, (coarse[...], fine[...]))
        for j in range(CJ):
            for i in range(CHUNK):
                for s in range(0, RANGES, 8):
                    start = s * step + (u * CJ + j) * CHUNK + i
                    out_ref[pl.ds(start, 8, stride=step), :] = solved[
                        j * RANGES + s : j * RANGES + s + 8, i * NK : (i + 1) * NK
                    ]


def final_kernel(inverse_ref, send_hbm, back_ref, out_hbm, send_ref, out_ref, sems):
    bring = pltpu.make_async_copy(send_hbm, send_ref, sems.at[V])
    bring.start()
    matrix = halves(inverse_ref[...])
    copies = []
    for v in range(V):
        lines = jnp.concatenate([back_ref[:, v, j].reshape(NI, NK) for j in range(CJ)], axis=1)
        solved = product(matrix, halves(lines))
        if v == 0:
            bring.wait()
        for j in range(CJ):
            for c in range(RANGES):
                x = send_ref[pl.ds((c * V + v) * SLAB + CJ + j, CHUNK, stride=CJ), :]
                out_ref[pl.ds(v * ROWS + c * CHUNK * CJ + j, CHUNK, stride=CJ), :] = (
                    x + solved[c * CHUNK : (c + 1) * CHUNK, j * NK : (j + 1) * NK]
                )
        rows = pl.ds(v * ROWS, ROWS)
        copies.append(pltpu.make_async_copy(out_ref.at[rows, :], out_hbm.at[rows, :], sems.at[v]))
        copies[-1].start()
    for copy in copies:
        copy.wait()


smem = pl.BlockSpec(memory_space=pltpu.SMEM)
vmem = pl.BlockSpec(memory_space=pltpu.VMEM)
hbm = pl.BlockSpec(memory_space=pltpu.HBM)


def run(kernel, specs, shapes, scratch, limit, *args, outs=None, more=None):
    one = not isinstance(shapes, list)
    shapes = [shapes] if one else shapes
    out = pl.pallas_call(
        kernel,
        out_shape=[jax.ShapeDtypeStruct(s, f32) for s in shapes],
        in_specs=specs,
        out_specs=outs or [vmem] * len(shapes),
        scratch_shapes=[pltpu.VMEM(s, t) for s, t in scratch] + (more or []),
        compiler_params=pltpu.CompilerParams(vmem_limit_bytes=limit << 20),
    )(*args)
    return out[0] if one else out


LANES = ((PIECES, SLOTS), jnp.int32)


def gather_call(cells, weights, st):
    scratch = [LANES, ((PIECES, SLOTS), f32), ((V * ROWS, NK), f32), LANES, ((DEPTH, NK), f32)]
    scratch += [((2, PIECES, NK), jnp.int32), ((2, PIECES, NK), f32), ((PIECES, 2, 8, NK), f32)]
    more = [pltpu.SMEM((PIECES, SLOTS), jnp.int32), pltpu.SemaphoreType.DMA((2 + V,))]
    shapes = [(PIECES, 1, V * SLOTS), (DEPTH, NK)]
    return run(gather_kernel, [hbm] * 3, shapes, scratch, 60, cells, weights, st, outs=[vmem, hbm], more=more)


def scatter_call(block, a, b, damp, cells, arrived, kept):
    count = PIECES - RANGES
    first = lax.broadcasted_iota(jnp.int32, (count, 1), 0) < block * RANGES
    offsets = (((jnp.where(first, cells[:count], cells[RANGES:]) >> 7) + PAD) * 8).T
    wide = (count * 8, 2 * NK)
    return run(
        scatter_kernel,
        [smem, smem, smem, smem, vmem, vmem, hbm],
        [(RANGES * V * SLAB, NK), (56, NK)],
        [((DEPTH, NK), f32), (wide, jnp.bfloat16), (wide, f32), (wide, f32)],
        48,
        offsets,
        a,
        b,
        damp,
        cells,
        arrived,
        kept,
        more=[pltpu.SemaphoreType.DMA],
    )


def slab_call(factors, inverse, lines):
    wide = ((NJ, CHUNK * NK), jnp.bfloat16)
    scratch = [((V, NJ * CHUNK, NK), f32), wide, wide]
    return run(slab_kernel, [vmem] * 3, (RANGES * V * CJ * CHUNK, NK), scratch, 20, factors, inverse, lines)


def final_call(inverse, send, back):
    back = back.reshape(RANGES, V, CJ, CHUNK, NK)
    scratch = [((RANGES * V * SLAB, NK), f32), ((V * ROWS, NK), f32)]
    more = [pltpu.SemaphoreType.DMA((V + 1,))]
    return run(final_kernel, [vmem, hbm, vmem], [(V * ROWS, NK)], scratch, 48, inverse, send, back, outs=[hbm], more=more)[0]


def exchange(x, axes):
    return lax.all_to_all(x, axes, split_axis=0, concat_axis=0, tiled=True)


def body(
    state,
    first_flux,
    second_flux,
    viscosity,
    first_inverse,
    second_inverse,
    donor_cell,
    donor_weight,
    receptor_cell,
):
    st = state.reshape(V * ROWS, NK)
    donated, kept = gather_call(donor_cell[0], donor_weight[0], st)
    arrived = exchange(donated, ("blk", "line"))
    block = lax.axis_index("blk")
    send, factors = scatter_call(block, first_flux, second_flux, viscosity, receptor_cell[0], arrived, kept)
    lines = exchange(send, "line")
    back = exchange(slab_call(factors, second_inverse[0], lines), "line")
    return final_call(first_inverse[0], send, back).reshape(1, V, NI, CJ, NK)


def solution(mesh):
    in_specs = (
        P("blk", None, None, "line", None),
        P("blk", None, None),
        P("blk", None, None),
        P("blk"),
        P("blk", None, None),
        P("blk", None, None),
        P(("blk", "line"), None, None),
        P(("blk", "line"), None, None),
        P(("blk", "line"), None, None),
    )
    out_specs = P("blk", None, None, "line", None)
    return jax.shard_map(body, mesh=mesh, in_specs=in_specs, out_specs=out_specs, check_vma=False)
```

```python
import jax
import jax.numpy as jnp
from jax import lax
from jax.experimental import pallas as pl
from jax.experimental.pallas import tpu as pltpu
from jax.sharding import PartitionSpec as P

V, NI, CJ, NK, PIECES, SLOTS, RANGES = 5, 256, 4, 128, 128, 128, 16
ROWS = NI * CJ
PAD = CJ
DEPTH = (ROWS + 2 * PAD) * 8
CHUNK = NI // RANGES
SLAB = (CHUNK + 2) * CJ
NJ = CJ * RANGES
f32 = jnp.float32


def others(block, n):
    return n + jnp.where(n >= block * RANGES, RANGES, 0)


def gather_kernel(cell_hbm, weight_hbm, st_hbm, out_ref, kept_ref, lane_ref, weight_ref, st_ref, offset_vmem, tiles, want, mix, picked, offset_ref, sems):
    copies = [
        pltpu.make_async_copy(cell_hbm, lane_ref, sems.at[0]),
        pltpu.make_async_copy(weight_hbm, weight_ref, sems.at[1]),
    ]
    for v in range(V):
        rows = pl.ds(v * ROWS, ROWS)
        copies.append(pltpu.make_async_copy(st_hbm.at[rows, :], st_ref.at[rows, :], sems.at[2 + v]))
    for copy in copies:
        copy.start()
    block = lax.axis_index("blk")
    lane = lax.broadcasted_iota(jnp.int32, (8, 128), 1)
    sub = lax.broadcasted_iota(jnp.int32, (8, 128), 0)
    odd = lane & 1
    half = lane >> 1
    even = (lane * 2) & 127
    copies[0].wait()
    offset_vmem[...] = ((lane_ref[...] >> 7) + PAD) * 8
    offsets = pltpu.make_async_copy(offset_vmem, offset_ref, sems.at[0])
    offsets.start()
    copies[1].wait()

    def before(b, carry):
        for t in range(4):
            r = pl.ds(pl.multiple_of(b * 32 + t * 8, 8), 8)
            cells = lane_ref[r, :] & 127
            weights = weight_ref[r, :]
            for h in range(2):
                want[h, r, :] = jnp.take_along_axis(cells, half + 64 * h, axis=1) + odd
                w = jnp.take_along_axis(weights, half + 64 * h, axis=1)
                mix[h, r, :] = jnp.where(odd == 0, w, 1.0 - w)
        return carry

    lax.fori_loop(0, PIECES // 32, before, 0)

    for t in range(PAD):
        tiles[t * 8 : t * 8 + 8, :] = jnp.zeros((8, 128), f32)
        tiles[DEPTH - t * 8 - 8 : DEPTH - t * 8, :] = jnp.zeros((8, 128), f32)
    for v in range(V):
        copies[2 + v].wait()

        def lay(b, carry):
            for t in range(8):
                c = b * 8 + t
                tiles[pl.ds(PAD * 8 + c * 64 + v, 8, stride=8), :] = st_ref[
                    pl.ds(pl.multiple_of(v * ROWS + c * 8, 8), 8), :
                ]
            return carry

        lax.fori_loop(0, ROWS // 64, lay, 0)
    keep = pltpu.make_async_copy(tiles, kept_ref, sems.at[2])
    keep.start()
    offsets.wait()

    def own(m, carry):
        for h in range(2):
            picked[block * RANGES + m, h] = jnp.zeros((8, 128), f32)
        return carry

    lax.fori_loop(0, RANGES, own, 0)

    def piece(k, carry):
        m = others(block, k)
        for h in range(2):
            index = jnp.broadcast_to(want[h, pl.ds(m, 1), :], (8, 128))
            acc = jnp.zeros((8, 128), f32)
            for q in range(64):
                x = tiles[pl.ds(pl.multiple_of(offset_ref[m, 64 * h + q], 8), 8), :]
                acc = jnp.where(half == q, jnp.take_along_axis(x, index, axis=1), acc)
            picked[m, h] = acc * jnp.broadcast_to(mix[h, pl.ds(m, 1), :], (8, 128))
        return carry

    lax.fori_loop(0, PIECES - RANGES, piece, 0, unroll=28)

    def after(b, carry):
        for t in range(16):
            sums = []
            for h in range(2):
                x = picked[b * 16 + t, h]
                x = x + pltpu.roll(x, 127, axis=1)
                sums.append(jnp.take_along_axis(x, even, axis=1))
            x = jnp.where(lane < 64, sums[0], sums[1])
            for v in range(V):
                out_ref[b * 16 + t, :, v * SLOTS : (v + 1) * SLOTS] = x[v : v + 1]
        return carry

    lax.fori_loop(0, PIECES // 16, after, 0)
    keep.wait()


def scatter_kernel(offset_vmem, a_ref, b_ref, damp_ref, cell_ref, arrived_ref, kept_ref, send_ref, factor_ref, tiles, parts, ping, pong, offset_ref, sem, offset_sem):
    offsets = pltpu.make_async_copy(offset_vmem, offset_ref, offset_sem)
    offsets.start()
    block = lax.axis_index("blk")
    keep = pltpu.make_async_copy(kept_ref, tiles, sem)
    keep.start()
    sub = lax.broadcasted_iota(jnp.int32, (8, 128), 0)

    def build(b, carry):
        r = pl.ds(pl.multiple_of(b * 16, 16), 16)
        x = []
        for t in range(2):
            n = others(block, 2 * b + t)
            lanes = (cell_ref[pl.ds(n, 1), :] & 127).astype(f32)
            values = jnp.broadcast_to(lanes, (8, 128))
            for v in range(V):
                row = arrived_ref[n, :, v * SLOTS : (v + 1) * SLOTS]
                values = jnp.where(sub == v, jnp.broadcast_to(row, (8, 128)), values)
            x.append(values)
        x = jnp.concatenate(x, axis=0)
        coarse = x.astype(jnp.bfloat16)
        parts[r, 0:128] = coarse
        parts[r, 128:256] = (x - coarse.astype(f32)).astype(jnp.bfloat16)
        return carry

    lax.fori_loop(0, (PIECES - RANGES) // 2, build, 0, unroll=4)
    for u in range(V):
        for v in range(V):
            factor_ref[u * V + v : u * V + v + 1, :] = jnp.full((1, 128), 0.5 * a_ref[0, u, v], f32)
            factor_ref[25 + u * V + v : 26 + u * V + v, :] = jnp.full((1, 128), 0.5 * b_ref[0, u, v], f32)
    factor_ref[50:51, :] = jnp.full((1, 128), damp_ref[0], f32)
    factor_ref[51:56, :] = jnp.zeros((5, 128), f32)
    lane = lax.broadcasted_iota(jnp.int32, (8, 128), 1).astype(f32)
    square = (2 * SLOTS, 2 * NK)
    code = (lax.broadcasted_iota(jnp.int32, square, 0) & 127) - (lax.broadcasted_iota(jnp.int32, square, 1) >> 7)
    group = (PIECES - RANGES) // 4

    def ones(pair):
        return jnp.where(code == 2 * pair, 1.0, 0.0).astype(jnp.bfloat16)

    def spread(mask, buffer, g):
        rows = slice(g * group * 8, (g + 1) * group * 8)
        buffer[rows, :] = jnp.dot(parts[rows, :], mask, preferred_element_type=f32)

    def put(pair, buffer, g):
        for n in range(g * group, (g + 1) * group):
            for c in range(2):
                columns = slice(c * 128, c * 128 + 128)
                offset = pl.multiple_of(offset_ref[2 * pair + c, n], 8)
                value = buffer[n * 8 : n * 8 + 8, columns]
                lanes = jnp.broadcast_to(buffer[n * 8 + V : n * 8 + V + 1, columns], (8, 128))
                pltpu.store(tiles.at[pl.ds(offset, 8), :], value, mask=lane == lanes)

    def step(pair, now, later):
        mask = ones(pair + 1)
        for g in range(4):
            spread(mask, later, g)
            put(pair, now, g)

    first = ones(0)
    for g in range(4):
        spread(first, ping, g)
    offsets.wait()
    keep.wait()

    def both(i, carry):
        step(2 * i, ping, pong)
        step(2 * i + 1, pong, ping)
        return carry

    lax.fori_loop(0, SLOTS // 4, both, 0)
    for t in range(PAD):
        tiles[(PAD + ROWS + t) * 8 : (PAD + ROWS + t + 1) * 8, :] = jnp.zeros((8, 128), f32)

    def slab(c, carry):
        for v in range(V):
            for t in range(0, SLAB, 8):
                send_ref[pl.ds(pl.multiple_of((c * V + v) * SLAB + t, 8), 8), :] = tiles[
                    pl.ds((c * CHUNK * CJ + t) * 8 + v, 8, stride=8), :
                ]
        return carry

    lax.fori_loop(0, RANGES, slab, 0)


def halves(x):
    coarse = x.astype(jnp.bfloat16)
    return coarse, (x - coarse.astype(f32)).astype(jnp.bfloat16)


def product(x, y):
    def dot(p, q):
        return jnp.dot(p, q, preferred_element_type=f32)

    return dot(x[0], y[0]) + (dot(x[0], y[1]) + dot(x[1], y[0]))


def slab_kernel(factor_ref, inverse_ref, in_ref, out_ref, rhs, wide):
    lane = lax.broadcasted_iota(jnp.int32, (CHUNK, 128), 1)

    def factor(r):
        return jnp.broadcast_to(factor_ref[r : r + 1, :], (CHUNK, 128))

    def one(s, carry):
        def cells(s, v, di, j):
            return in_ref[pl.ds((s * V + v) * SLAB + (1 + di) * CJ + j, CHUNK, stride=CJ), :]

        for j in range(CJ):
            di, dj, lap = [], [], []
            for v in range(V):
                c = cells(s, v, 0, j)
                im = cells(s, v, -1, j)
                ip = cells(s, v, 1, j)
                if j == 0:
                    jm = jnp.where(s > 0, cells(jnp.maximum(s - 1, 0), v, 0, CJ - 1), 0.0)
                else:
                    jm = cells(s, v, 0, j - 1)
                if j == CJ - 1:
                    jp = jnp.where(s < RANGES - 1, cells(jnp.minimum(s + 1, RANGES - 1), v, 0, 0), 0.0)
                else:
                    jp = cells(s, v, 0, j + 1)
                kp = jnp.where(lane == NK - 1, 0.0, pltpu.roll(c, NK - 1, axis=1))
                km = jnp.where(lane == 0, 0.0, pltpu.roll(c, 1, axis=1))
                lap.append(ip + im + jp + jm + kp + km - 6.0 * c)
                di.append(ip - im)
                dj.append(jp - jm)
            for u in range(V):
                r = factor(50) * lap[u]
                for v in range(V):
                    r = r - (factor(u * V + v) * di[v] + factor(25 + u * V + v) * dj[v])
                rhs[u, pl.ds(pl.multiple_of((s * CJ + j) * CHUNK, CHUNK), CHUNK), :] = r
        return carry

    lax.fori_loop(0, RANGES, one, 0, unroll=2)
    matrix = halves(jnp.concatenate([inverse_ref[pl.ds(j, RANGES, stride=CJ), :] for j in range(CJ)], axis=0))
    matrix = jnp.concatenate([matrix[0], matrix[0], matrix[1]], axis=1)
    step = V * CJ * CHUNK
    for u in range(V):
        for i in range(CHUNK):
            columns = slice(i * NK, (i + 1) * NK)
            coarse, fine = halves(rhs[u, pl.ds(i, NJ, stride=CHUNK), :])
            wide[0:NJ, columns] = coarse
            wide[NJ : 2 * NJ, columns] = fine
            wide[2 * NJ : 3 * NJ, columns] = coarse
        solved = jnp.dot(matrix, wide[...], preferred_element_type=f32)
        for j in range(CJ):
            for i in range(CHUNK):
                for s in range(0, RANGES, 8):
                    start = s * step + (u * CJ + j) * CHUNK + i
                    out_ref[pl.ds(start, 8, stride=step), :] = solved[
                        j * RANGES + s : j * RANGES + s + 8, i * NK : (i + 1) * NK
                    ]


def final_kernel(inverse_ref, send_hbm, back_ref, out_hbm, send_ref, out_ref, sems):
    bring = pltpu.make_async_copy(send_hbm, send_ref, sems.at[V])
    bring.start()
    matrix = halves(inverse_ref[...])
    copies = []
    for v in range(V):
        lines = jnp.concatenate([back_ref[:, v, j].reshape(NI, NK) for j in range(CJ)], axis=1)
        solved = product(matrix, halves(lines))
        if v == 0:
            bring.wait()
        for j in range(CJ):
            for c in range(RANGES):
                x = send_ref[pl.ds((c * V + v) * SLAB + CJ + j, CHUNK, stride=CJ), :]
                out_ref[pl.ds(v * ROWS + c * CHUNK * CJ + j, CHUNK, stride=CJ), :] = (
                    x + solved[c * CHUNK : (c + 1) * CHUNK, j * NK : (j + 1) * NK]
                )
        rows = pl.ds(v * ROWS, ROWS)
        copies.append(pltpu.make_async_copy(out_ref.at[rows, :], out_hbm.at[rows, :], sems.at[v]))
        copies[-1].start()
    for copy in copies:
        copy.wait()


smem = pl.BlockSpec(memory_space=pltpu.SMEM)
vmem = pl.BlockSpec(memory_space=pltpu.VMEM)
hbm = pl.BlockSpec(memory_space=pltpu.HBM)


def run(kernel, specs, shapes, scratch, limit, *args, outs=None, more=None):
    one = not isinstance(shapes, list)
    shapes = [shapes] if one else shapes
    out = pl.pallas_call(
        kernel,
        out_shape=[jax.ShapeDtypeStruct(s, f32) for s in shapes],
        in_specs=specs,
        out_specs=outs or [vmem] * len(shapes),
        scratch_shapes=[pltpu.VMEM(s, t) for s, t in scratch] + (more or []),
        compiler_params=pltpu.CompilerParams(vmem_limit_bytes=limit << 20),
    )(*args)
    return out[0] if one else out


LANES = ((PIECES, SLOTS), jnp.int32)


def gather_call(cells, weights, st):
    scratch = [LANES, ((PIECES, SLOTS), f32), ((V * ROWS, NK), f32), LANES, ((DEPTH, NK), f32)]
    scratch += [((2, PIECES, NK), jnp.int32), ((2, PIECES, NK), f32), ((PIECES, 2, 8, NK), f32)]
    more = [pltpu.SMEM((PIECES, SLOTS), jnp.int32), pltpu.SemaphoreType.DMA((2 + V,))]
    shapes = [(PIECES, 1, V * SLOTS), (DEPTH, NK)]
    return run(gather_kernel, [hbm] * 3, shapes, scratch, 60, cells, weights, st, outs=[vmem, hbm], more=more)


def scatter_call(block, a, b, damp, cells, arrived, kept):
    count = PIECES - RANGES
    first = lax.broadcasted_iota(jnp.int32, (PIECES, 1), 0) < block * RANGES
    shifted = jnp.concatenate([cells[RANGES:], cells[:RANGES]])
    offsets = (((jnp.where(first, cells, shifted) >> 7) + PAD) * 8).T
    wide = (count * 8, 2 * NK)
    return run(
        scatter_kernel,
        [vmem, smem, smem, smem, vmem, vmem, hbm],
        [(RANGES * V * SLAB, NK), (56, NK)],
        [((DEPTH, NK), f32), (wide, jnp.bfloat16), (wide, f32), (wide, f32)],
        48,
        offsets,
        a,
        b,
        damp,
        cells,
        arrived,
        kept,
        more=[pltpu.SMEM((SLOTS, PIECES), jnp.int32), pltpu.SemaphoreType.DMA, pltpu.SemaphoreType.DMA],
    )


def slab_call(factors, inverse, lines):
    scratch = [((V, NJ * CHUNK, NK), f32), ((3 * NJ, CHUNK * NK), jnp.bfloat16)]
    return run(slab_kernel, [vmem] * 3, (RANGES * V * CJ * CHUNK, NK), scratch, 20, factors, inverse, lines)


def final_call(inverse, send, back):
    back = back.reshape(RANGES, V, CJ, CHUNK, NK)
    scratch = [((RANGES * V * SLAB, NK), f32), ((V * ROWS, NK), f32)]
    more = [pltpu.SemaphoreType.DMA((V + 1,))]
    return run(final_kernel, [vmem, hbm, vmem], [(V * ROWS, NK)], scratch, 48, inverse, send, back, outs=[hbm], more=more)[0]


def exchange(x, axes):
    return lax.all_to_all(x, axes, split_axis=0, concat_axis=0, tiled=True)


def body(
    state,
    first_flux,
    second_flux,
    viscosity,
    first_inverse,
    second_inverse,
    donor_cell,
    donor_weight,
    receptor_cell,
):
    st = state.reshape(V * ROWS, NK)
    donated, kept = gather_call(donor_cell[0], donor_weight[0], st)
    arrived = exchange(donated, ("blk", "line"))
    block = lax.axis_index("blk")
    send, factors = scatter_call(block, first_flux, second_flux, viscosity, receptor_cell[0], arrived, kept)
    lines = exchange(send, "line")
    back = exchange(slab_call(factors, second_inverse[0], lines), "line")
    return final_call(first_inverse[0], send, back).reshape(1, V, NI, CJ, NK)


def solution(mesh):
    in_specs = (
        P("blk", None, None, "line", None),
        P("blk", None, None),
        P("blk", None, None),
        P("blk"),
        P("blk", None, None),
        P("blk", None, None),
        P(("blk", "line"), None, None),
        P(("blk", "line"), None, None),
        P(("blk", "line"), None, None),
    )
    out_specs = P("blk", None, None, "line", None)
    return jax.shard_map(body, mesh=mesh, in_specs=in_specs, out_specs=out_specs, check_vma=False)
```

```python
import jax
import jax.numpy as jnp
from jax import lax
from jax.experimental import pallas as pl
from jax.experimental.pallas import tpu as pltpu
from jax.sharding import PartitionSpec as P

V, NI, CJ, NK, PIECES, SLOTS, RANGES = 5, 256, 4, 128, 128, 128, 16
ROWS = NI * CJ
PAD = CJ
DEPTH = (ROWS + 2 * PAD) * 8
CHUNK = NI // RANGES
SLAB = (CHUNK + 2) * CJ
NJ = CJ * RANGES
f32 = jnp.float32


def others(block, n):
    return n + jnp.where(n >= block * RANGES, RANGES, 0)


def gather_kernel(cell_hbm, weight_hbm, st_hbm, out_ref, kept_ref, lane_ref, weight_ref, st_ref, offset_vmem, tiles, want, mix, picked, offset_ref, sems):
    copies = [
        pltpu.make_async_copy(cell_hbm, lane_ref, sems.at[0]),
        pltpu.make_async_copy(weight_hbm, weight_ref, sems.at[1]),
    ]
    for v in range(V):
        rows = pl.ds(v * ROWS, ROWS)
        copies.append(pltpu.make_async_copy(st_hbm.at[rows, :], st_ref.at[rows, :], sems.at[2 + v]))
    for copy in copies:
        copy.start()
    block = lax.axis_index("blk")
    lane = lax.broadcasted_iota(jnp.int32, (8, 128), 1)
    sub = lax.broadcasted_iota(jnp.int32, (8, 128), 0)
    odd = lane & 1
    half = lane >> 1
    even = (lane * 2) & 127
    copies[0].wait()
    offset_vmem[...] = ((lane_ref[...] >> 7) + PAD) * 8
    offsets = pltpu.make_async_copy(offset_vmem, offset_ref, sems.at[0])
    offsets.start()
    copies[1].wait()

    def before(b, carry):
        for t in range(4):
            r = pl.ds(pl.multiple_of(b * 32 + t * 8, 8), 8)
            cells = lane_ref[r, :] & 127
            weights = weight_ref[r, :]
            for h in range(2):
                want[h, r, :] = jnp.take_along_axis(cells, half + 64 * h, axis=1) + odd
                w = jnp.take_along_axis(weights, half + 64 * h, axis=1)
                mix[h, r, :] = jnp.where(odd == 0, w, 1.0 - w)
        return carry

    lax.fori_loop(0, PIECES // 32, before, 0)

    for t in range(PAD):
        tiles[t * 8 : t * 8 + 8, :] = jnp.zeros((8, 128), f32)
        tiles[DEPTH - t * 8 - 8 : DEPTH - t * 8, :] = jnp.zeros((8, 128), f32)
    for v in range(V):
        copies[2 + v].wait()

        def lay(b, carry):
            for t in range(8):
                c = b * 8 + t
                tiles[pl.ds(PAD * 8 + c * 64 + v, 8, stride=8), :] = st_ref[
                    pl.ds(pl.multiple_of(v * ROWS + c * 8, 8), 8), :
                ]
            return carry

        lax.fori_loop(0, ROWS // 64, lay, 0)
    keep = pltpu.make_async_copy(tiles, kept_ref, sems.at[2])
    keep.start()
    offsets.wait()

    def own(m, carry):
        for h in range(2):
            picked[block * RANGES + m, h] = jnp.zeros((8, 128), f32)
        return carry

    lax.fori_loop(0, RANGES, own, 0)

    def piece(k, carry):
        m = others(block, k)
        for h in range(2):
            index = jnp.broadcast_to(want[h, pl.ds(m, 1), :], (8, 128))
            acc = jnp.zeros((8, 128), f32)
            for q in range(64):
                x = tiles[pl.ds(pl.multiple_of(offset_ref[m, 64 * h + q], 8), 8), :]
                acc = jnp.where(half == q, jnp.take_along_axis(x, index, axis=1), acc)
            picked[m, h] = acc * jnp.broadcast_to(mix[h, pl.ds(m, 1), :], (8, 128))
        return carry

    lax.fori_loop(0, PIECES - RANGES, piece, 0, unroll=28)

    def after(b, carry):
        for t in range(16):
            sums = []
            for h in range(2):
                x = picked[b * 16 + t, h]
                x = x + pltpu.roll(x, 127, axis=1)
                sums.append(jnp.take_along_axis(x, even, axis=1))
            x = jnp.where(lane < 64, sums[0], sums[1])
            for v in range(V):
                out_ref[b * 16 + t, :, v * SLOTS : (v + 1) * SLOTS] = x[v : v + 1]
        return carry

    lax.fori_loop(0, PIECES // 16, after, 0)
    keep.wait()


def scatter_kernel(offset_vmem, a_ref, b_ref, damp_ref, cell_ref, arrived_ref, kept_ref, send_ref, factor_ref, tiles, parts, ping, pong, offset_ref, sem, offset_sem):
    offsets = pltpu.make_async_copy(offset_vmem, offset_ref, offset_sem)
    offsets.start()
    block = lax.axis_index("blk")
    keep = pltpu.make_async_copy(kept_ref, tiles, sem)
    keep.start()
    sub = lax.broadcasted_iota(jnp.int32, (8, 128), 0)

    def build(b, carry):
        r = pl.ds(pl.multiple_of(b * 16, 16), 16)
        x = []
        for t in range(2):
            n = others(block, 2 * b + t)
            lanes = (cell_ref[pl.ds(n, 1), :] & 127).astype(f32)
            values = jnp.broadcast_to(lanes, (8, 128))
            for v in range(V):
                row = arrived_ref[n, :, v * SLOTS : (v + 1) * SLOTS]
                values = jnp.where(sub == v, jnp.broadcast_to(row, (8, 128)), values)
            x.append(values)
        x = jnp.concatenate(x, axis=0)
        coarse = x.astype(jnp.bfloat16)
        parts[r, 0:128] = coarse
        parts[r, 128:256] = (x - coarse.astype(f32)).astype(jnp.bfloat16)
        return carry

    lax.fori_loop(0, (PIECES - RANGES) // 2, build, 0, unroll=4)
    for u in range(V):
        for v in range(V):
            factor_ref[u * V + v : u * V + v + 1, :] = jnp.full((1, 128), 0.5 * a_ref[0, u, v], f32)
            factor_ref[25 + u * V + v : 26 + u * V + v, :] = jnp.full((1, 128), 0.5 * b_ref[0, u, v], f32)
    factor_ref[50:51, :] = jnp.full((1, 128), damp_ref[0], f32)
    factor_ref[51:56, :] = jnp.zeros((5, 128), f32)
    lane = lax.broadcasted_iota(jnp.int32, (8, 128), 1).astype(f32)
    square = (2 * SLOTS, 2 * NK)
    code = (lax.broadcasted_iota(jnp.int32, square, 0) & 127) - (lax.broadcasted_iota(jnp.int32, square, 1) >> 7)
    group = (PIECES - RANGES) // 4

    def ones(pair):
        return jnp.where(code == 2 * pair, 1.0, 0.0).astype(jnp.bfloat16)

    def spread(mask, buffer, g):
        rows = slice(g * group * 8, (g + 1) * group * 8)
        buffer[rows, :] = jnp.dot(parts[rows, :], mask, preferred_element_type=f32)

    def put(pair, buffer, g):
        for n in range(g * group, (g + 1) * group):
            for c in range(2):
                columns = slice(c * 128, c * 128 + 128)
                offset = pl.multiple_of(offset_ref[2 * pair + c, n], 8)
                value = buffer[n * 8 : n * 8 + 8, columns]
                lanes = jnp.broadcast_to(buffer[n * 8 + V : n * 8 + V + 1, columns], (8, 128))
                pltpu.store(tiles.at[pl.ds(offset, 8), :], value, mask=lane == lanes)

    def step(pair, now, later):
        mask = ones(pair + 1)
        for g in range(4):
            spread(mask, later, g)
            put(pair, now, g)

    first = ones(0)
    for g in range(4):
        spread(first, ping, g)
    offsets.wait()
    keep.wait()

    def both(i, carry):
        step(2 * i, ping, pong)
        step(2 * i + 1, pong, ping)
        return carry

    lax.fori_loop(0, SLOTS // 4, both, 0)
    for t in range(PAD):
        tiles[(PAD + ROWS + t) * 8 : (PAD + ROWS + t + 1) * 8, :] = jnp.zeros((8, 128), f32)

    def slab(c, carry):
        for v in range(V):
            for t in range(0, SLAB, 8):
                send_ref[pl.ds(pl.multiple_of((c * V + v) * SLAB + t, 8), 8), :] = tiles[
                    pl.ds((c * CHUNK * CJ + t) * 8 + v, 8, stride=8), :
                ]
        return carry

    lax.fori_loop(0, RANGES, slab, 0, unroll=2)


def halves(x):
    coarse = x.astype(jnp.bfloat16)
    return coarse, (x - coarse.astype(f32)).astype(jnp.bfloat16)


def product(x, y):
    def dot(p, q):
        return jnp.dot(p, q, preferred_element_type=f32)

    return dot(x[0], y[0]) + (dot(x[0], y[1]) + dot(x[1], y[0]))


def slab_kernel(factor_ref, inverse_ref, in_ref, out_ref, rhs, wide):
    lane = lax.broadcasted_iota(jnp.int32, (CHUNK, 128), 1)

    def factor(r):
        return jnp.broadcast_to(factor_ref[r : r + 1, :], (CHUNK, 128))

    def one(s, carry):
        def cells(s, v, di, j):
            return in_ref[pl.ds((s * V + v) * SLAB + (1 + di) * CJ + j, CHUNK, stride=CJ), :]

        for j in range(CJ):
            di, dj, lap = [], [], []
            for v in range(V):
                c = cells(s, v, 0, j)
                im = cells(s, v, -1, j)
                ip = cells(s, v, 1, j)
                if j == 0:
                    jm = jnp.where(s > 0, cells(jnp.maximum(s - 1, 0), v, 0, CJ - 1), 0.0)
                else:
                    jm = cells(s, v, 0, j - 1)
                if j == CJ - 1:
                    jp = jnp.where(s < RANGES - 1, cells(jnp.minimum(s + 1, RANGES - 1), v, 0, 0), 0.0)
                else:
                    jp = cells(s, v, 0, j + 1)
                kp = jnp.where(lane == NK - 1, 0.0, pltpu.roll(c, NK - 1, axis=1))
                km = jnp.where(lane == 0, 0.0, pltpu.roll(c, 1, axis=1))
                lap.append(ip + im + jp + jm + kp + km - 6.0 * c)
                di.append(ip - im)
                dj.append(jp - jm)
            for u in range(V):
                r = factor(50) * lap[u]
                for v in range(V):
                    r = r - (factor(u * V + v) * di[v] + factor(25 + u * V + v) * dj[v])
                rhs[u, pl.ds(pl.multiple_of((s * CJ + j) * CHUNK, CHUNK), CHUNK), :] = r
        return carry

    lax.fori_loop(0, RANGES, one, 0, unroll=4)
    matrix = halves(jnp.concatenate([inverse_ref[pl.ds(j, RANGES, stride=CJ), :] for j in range(CJ)], axis=0))
    matrix = jnp.concatenate([matrix[0], matrix[0], matrix[1]], axis=1)
    step = V * CJ * CHUNK
    for u in range(V):
        for i in range(CHUNK):
            columns = slice(i * NK, (i + 1) * NK)
            coarse, fine = halves(rhs[u, pl.ds(i, NJ, stride=CHUNK), :])
            wide[0:NJ, columns] = coarse
            wide[NJ : 2 * NJ, columns] = fine
            wide[2 * NJ : 3 * NJ, columns] = coarse
        solved = jnp.dot(matrix, wide[...], preferred_element_type=f32)
        for j in range(CJ):
            for i in range(CHUNK):
                for s in range(0, RANGES, 8):
                    start = s * step + (u * CJ + j) * CHUNK + i
                    out_ref[pl.ds(start, 8, stride=step), :] = solved[
                        j * RANGES + s : j * RANGES + s + 8, i * NK : (i + 1) * NK
                    ]


def final_kernel(inverse_ref, send_hbm, back_ref, out_hbm, send_ref, out_ref, sems):
    bring = pltpu.make_async_copy(send_hbm, send_ref, sems.at[V])
    bring.start()
    matrix = halves(inverse_ref[...])
    copies = []
    for v in range(V):
        lines = jnp.concatenate([back_ref[:, v, j].reshape(NI, NK) for j in range(CJ)], axis=1)
        solved = product(matrix, halves(lines))
        if v == 0:
            bring.wait()
        for j in range(CJ):
            for c in range(RANGES):
                x = send_ref[pl.ds((c * V + v) * SLAB + CJ + j, CHUNK, stride=CJ), :]
                out_ref[pl.ds(v * ROWS + c * CHUNK * CJ + j, CHUNK, stride=CJ), :] = (
                    x + solved[c * CHUNK : (c + 1) * CHUNK, j * NK : (j + 1) * NK]
                )
        rows = pl.ds(v * ROWS, ROWS)
        copies.append(pltpu.make_async_copy(out_ref.at[rows, :], out_hbm.at[rows, :], sems.at[v]))
        copies[-1].start()
    for copy in copies:
        copy.wait()


smem = pl.BlockSpec(memory_space=pltpu.SMEM)
vmem = pl.BlockSpec(memory_space=pltpu.VMEM)
hbm = pl.BlockSpec(memory_space=pltpu.HBM)


def run(kernel, specs, shapes, scratch, limit, *args, outs=None, more=None):
    one = not isinstance(shapes, list)
    shapes = [shapes] if one else shapes
    out = pl.pallas_call(
        kernel,
        out_shape=[jax.ShapeDtypeStruct(s, f32) for s in shapes],
        in_specs=specs,
        out_specs=outs or [vmem] * len(shapes),
        scratch_shapes=[pltpu.VMEM(s, t) for s, t in scratch] + (more or []),
        compiler_params=pltpu.CompilerParams(vmem_limit_bytes=limit << 20),
    )(*args)
    return out[0] if one else out


LANES = ((PIECES, SLOTS), jnp.int32)


def gather_call(cells, weights, st):
    scratch = [LANES, ((PIECES, SLOTS), f32), ((V * ROWS, NK), f32), LANES, ((DEPTH, NK), f32)]
    scratch += [((2, PIECES, NK), jnp.int32), ((2, PIECES, NK), f32), ((PIECES, 2, 8, NK), f32)]
    more = [pltpu.SMEM((PIECES, SLOTS), jnp.int32), pltpu.SemaphoreType.DMA((2 + V,))]
    shapes = [(PIECES, 1, V * SLOTS), (DEPTH, NK)]
    return run(gather_kernel, [hbm] * 3, shapes, scratch, 60, cells, weights, st, outs=[vmem, hbm], more=more)


def scatter_call(block, a, b, damp, cells, arrived, kept):
    count = PIECES - RANGES
    first = lax.broadcasted_iota(jnp.int32, (PIECES, 1), 0) < block * RANGES
    shifted = jnp.concatenate([cells[RANGES:], cells[:RANGES]])
    offsets = (((jnp.where(first, cells, shifted) >> 7) + PAD) * 8).T
    wide = (count * 8, 2 * NK)
    return run(
        scatter_kernel,
        [vmem, smem, smem, smem, vmem, vmem, hbm],
        [(RANGES * V * SLAB, NK), (56, NK)],
        [((DEPTH, NK), f32), (wide, jnp.bfloat16), (wide, f32), (wide, f32)],
        48,
        offsets,
        a,
        b,
        damp,
        cells,
        arrived,
        kept,
        more=[pltpu.SMEM((SLOTS, PIECES), jnp.int32), pltpu.SemaphoreType.DMA, pltpu.SemaphoreType.DMA],
    )


def slab_call(factors, inverse, lines):
    scratch = [((V, NJ * CHUNK, NK), f32), ((3 * NJ, CHUNK * NK), jnp.bfloat16)]
    return run(slab_kernel, [vmem] * 3, (RANGES * V * CJ * CHUNK, NK), scratch, 20, factors, inverse, lines)


def final_call(inverse, send, back):
    back = back.reshape(RANGES, V, CJ, CHUNK, NK)
    scratch = [((RANGES * V * SLAB, NK), f32), ((V * ROWS, NK), f32)]
    more = [pltpu.SemaphoreType.DMA((V + 1,))]
    return run(final_kernel, [vmem, hbm, vmem], [(V * ROWS, NK)], scratch, 48, inverse, send, back, outs=[hbm], more=more)[0]


def exchange(x, axes):
    return lax.all_to_all(x, axes, split_axis=0, concat_axis=0, tiled=True)


def body(
    state,
    first_flux,
    second_flux,
    viscosity,
    first_inverse,
    second_inverse,
    donor_cell,
    donor_weight,
    receptor_cell,
):
    st = state.reshape(V * ROWS, NK)
    donated, kept = gather_call(donor_cell[0], donor_weight[0], st)
    arrived = exchange(donated, ("blk", "line"))
    block = lax.axis_index("blk")
    send, factors = scatter_call(block, first_flux, second_flux, viscosity, receptor_cell[0], arrived, kept)
    lines = exchange(send, "line")
    back = exchange(slab_call(factors, second_inverse[0], lines), "line")
    return final_call(first_inverse[0], send, back).reshape(1, V, NI, CJ, NK)


def solution(mesh):
    in_specs = (
        P("blk", None, None, "line", None),
        P("blk", None, None),
        P("blk", None, None),
        P("blk"),
        P("blk", None, None),
        P("blk", None, None),
        P(("blk", "line"), None, None),
        P(("blk", "line"), None, None),
        P(("blk", "line"), None, None),
    )
    out_specs = P("blk", None, None, "line", None)
    return jax.shard_map(body, mesh=mesh, in_specs=in_specs, out_specs=out_specs, check_vma=False)
```
